32 devices in a mesh: row: 4 (over y, x), col: 8 (over z, core).
Axes of the slice: x: 2, y: 2, z: 4, core: 2. Of those that a mesh axis runs over, the one named last changes fastest.
Arguments:
- inputs: bfloat16 [4, 64, 64, 1280], P(None, 'row', 'col'), may hold values from -6 to 6
- cotangent: bfloat16 [4, 64, 64, 1280], P(None, 'row', 'col'), may hold values from -6 to 6
- w_in: bfloat16 [1474560], P(('row', 'col')), may hold values from -0.0546875 to 0.0546875
- w_out: bfloat16 [1474560], P(('row', 'col')), may hold values from -0.1875 to 0.1875
Outputs:
- input_grad: bfloat16 [4, 64, 64, 1280], P(None, 'row', 'col')
The draws below stay inside these ranges and needn't reach their ends.
All inputs are finite; a program needn't handle non-finite values.
Results may differ from the reference program's by a relative error of at most 0.0032.
Values may be sent and summed in bfloat16 or wider, within the bound.
No kernel may reach another device: no remote copies, remote signals or barrier semaphores. Data moves between devices by JAX's collectives and lax.ppermute only.
A program may use at most 64 MiB of HBM per device.

```python
import jax
import jax.numpy as jnp
from jax import lax

C = 1280
MID = 128
BATCH = 4
HEIGHT = 64
WIDTH = 64


def block_levels(rng, extent, shards, least, largest):
    def one(position, blocks):
        heights = jax.random.uniform(jax.random.fold_in(jax.random.fold_in(rng, 6), position), (blocks,), jnp.float32, least / len(shards), largest / len(shards))
        return jnp.repeat(jnp.exp(heights), extent[position] // blocks).reshape((-1,) + (1,) * (len(extent) - position - 1))

    loudness = one(*shards[0])
    for cut in shards[1:]:
        loudness = loudness * one(*cut)
    return loudness


def scatter_about(stream_key, dims, scale, bound, pieces=(), held_as=jnp.bfloat16):
    drawn = scale * jax.random.normal(stream_key, dims, jnp.float32)
    if pieces:
        drawn = drawn * block_levels(stream_key, dims, pieces, -0.22, 0.18)
    return jnp.clip(drawn, -bound, bound).astype(held_as)


def setup_inputs(seed: int = 0) -> dict:
    arg_keys = jax.random.split(jax.random.key(seed), 5)
    inputs = scatter_about(arg_keys[0], (BATCH, HEIGHT, WIDTH, C), 1.0, 6.0, ((1, 4), (2, 8)))
    cotangent = scatter_about(arg_keys[1], (BATCH, HEIGHT, WIDTH, C), 1.0, 6.0, ((1, 4), (2, 8)))
    w_in = scatter_about(arg_keys[2], (9 * C * MID,), (9 * C) ** -0.5, 0.0546875, ((0, 32),))
    w_out = scatter_about(arg_keys[3], (9 * MID * C,), (9 * MID) ** -0.5, 0.1875, ((0, 32),))
    return dict(inputs=inputs, cotangent=cotangent, w_in=w_in, w_out=w_out)


def convolve(padded, kernel):
    return lax.conv_general_dilated(padded.astype(jnp.float32), kernel.astype(jnp.float32), (1, 1), "VALID", dimension_numbers=("NHWC", "HWIO", "NHWC"), precision=lax.Precision.HIGHEST)


def border(image):
    return jnp.pad(image[None], ((0, 0), (1, 1), (1, 1), (0, 0)))


def reference(inputs, cotangent, w_in, w_out):
    ker_in = w_in.reshape(3, 3, C, MID)
    ker_out = w_out.reshape(3, 3, MID, C)
    out_back = ker_out[::-1, ::-1].transpose(0, 1, 3, 2)
    in_back = ker_in[::-1, ::-1].transpose(0, 1, 3, 2)

    def single(pair):
        image, grad_image = pair
        pre = convolve(border(image), ker_in)[0]
        back_mid = convolve(border(grad_image), out_back)[0]
        sig = jax.nn.sigmoid(pre)
        grad_mid = (back_mid * (sig * (1.0 + pre * (1.0 - sig)))).astype(jnp.bfloat16)
        result = grad_image.astype(jnp.float32) + convolve(border(grad_mid), in_back)[0]
        return result.astype(jnp.bfloat16)

    return lax.map(single, (inputs, cotangent))
```

```python
import jax
import jax.numpy as jnp
from jax import lax
from jax.experimental import pallas as pl
from jax.experimental.pallas import tpu as pltpu
from jax.sharding import PartitionSpec as P

AXES = ("row", "col")
VMEM_LIMIT = 40 * 1024 * 1024
TAPS = 3


def is_power(n):
    return n > 0 and n & (n - 1) == 0


def whole(array):
    return pl.BlockSpec(memory_space=pltpu.VMEM)


def anywhere(array):
    return pl.BlockSpec(memory_space=pl.ANY)


class Geometry:
    def __init__(self, inputs, w_in):
        self.batch, self.high, self.wide, self.chan = inputs.shape
        self.rows, self.cols = lax.axis_size("row"), lax.axis_size("col")
        self.zs = self.cols // 2
        self.shard = w_in.shape[0]
        self.mid = self.shard * self.rows * self.cols // (TAPS * TAPS * self.chan)
        self.pixels = self.batch * self.high * self.wide
        self.ext = self.high + 2
        self.lines = self.batch * self.ext
        self.plane = self.lines * self.wide
        self.unit = 2 * self.shard // self.mid

    def pieces_fit(self):
        return (
            self.cols % 2 == 0
            and is_power(self.zs)
            and is_power(self.rows)
            and self.rows >= 2
            and self.shard % self.chan == 0
            and self.shard % self.mid == 0
            and self.unit % 16 == 0
            and self.chan % self.mid == 0
            and (2 * self.shard // self.chan) % 8 == 0
        )


def device_perm(geo, move):
    pairs = []
    for row in range(geo.rows):
        for col in range(geo.cols):
            r, z, k = move(row, col // 2, col % 2)
            pairs.append((row * geo.cols + col, r * geo.cols + z * 2 + k))
    return pairs


def send(x, perm):
    return lax.ppermute(x, AXES, perm)


def row_bits(geo, core):
    bits = [1 << i for i in range(geo.rows.bit_length() - 1)]
    return bits if core == 0 else bits[::-1]


def row_masks(geo, core):
    masks = [0]
    for bit in row_bits(geo, core):
        masks = masks + [m ^ bit for m in masks]
    return masks


def gather_rows(geo, x):
    parts = [x]
    for step in range(len(row_bits(geo, 0))):
        held = parts[0] if len(parts) == 1 else jnp.concatenate(parts, axis=0)
        perm = device_perm(
            geo, lambda r, z, k: (r ^ row_bits(geo, k)[step], z, k)
        )
        parts = [held, send(held, perm)]
    return parts


def gather_pieces(geo, w_in, w_out, core):
    blocks = geo.chan // geo.mid
    deep = geo.shard // geo.chan
    k1 = w_in.reshape(-1, geo.mid)
    k2 = w_out.reshape(deep, blocks, geo.mid).transpose(1, 0, 2)
    swap = device_perm(geo, lambda r, z, k: (r, z, 1 - k))
    got = send(jnp.where(core == 0, k2.reshape(-1, geo.mid), k1), swap)
    chip1 = jnp.concatenate([k1, got], axis=0)
    chip2 = jnp.concatenate([got.reshape(blocks, deep, geo.mid), k2], axis=1)
    own = jnp.where(core == 0, chip1, chip2.reshape(-1, geo.mid))
    ours = []
    for dz in range(geo.zs):
        here = own if dz == 0 else send(own, device_perm(geo, lambda r, z, k: (r, z ^ dz, k)))
        ours.append(gather_rows(geo, here))
    theirs = [[send(x, swap) for x in parts] for parts in ours]
    flat_ours = [x for parts in ours for x in parts]
    flat_theirs = [x for parts in theirs for x in parts]
    return flat_ours, flat_theirs


def chip_table(geo, core):
    row = lax.axis_index("row")
    z = lax.axis_index("col") // 2
    dz = jnp.arange(geo.zs)[:, None]
    by_core = [
        ((row ^ jnp.array(row_masks(geo, k))[None, :]) * geo.zs + (z ^ dz)).reshape(-1)
        for k in (0, 1)
    ]
    mine = jnp.where(core == 0, by_core[0], by_core[1])
    other = jnp.where(core == 0, by_core[1], by_core[0])
    return jnp.concatenate([jnp.asarray([core]), mine, other]).astype(jnp.int32)


def assemble(geo, table, ours, theirs, k1s, k2st, k2s, sems):
    unit = geo.unit
    core = table[0]
    jobs = []
    count = 0
    for source, group in enumerate((ours, theirs)):
        for ref in group:
            for q in range(ref.shape[0] // unit):
                jobs.append((source, ref.at[pl.ds(q * unit, unit)], count))
                count += 1

    def copies(job):
        source, ref, index = job
        chip = table[1 + index]
        first = pltpu.make_async_copy(
            ref, k1s.at[pl.ds(pl.multiple_of(chip * unit, 16), unit)], sems.at[index]
        )
        second = pltpu.make_async_copy(ref, k2st.at[chip], sems.at[index])
        return first, second, core == source

    for job in jobs:
        first, second, is_first = copies(job)
        pl.when(is_first)(first.start)
        pl.when(jnp.logical_not(is_first))(second.start)
    for job in jobs:
        first, second, is_first = copies(job)
        pl.when(is_first)(first.wait)
        pl.when(jnp.logical_not(is_first))(second.wait)
    blocks = geo.chan // geo.mid
    deep = 2 * geo.shard // geo.chan
    for s in range(geo.rows * geo.zs):
        for b in range(blocks):
            k2s[s * deep : (s + 1) * deep, b * geo.mid : (b + 1) * geo.mid] = k2st[
                s, b * deep : (b + 1) * deep, :
            ]


def partial_convolutions(geo, k1s, k2s, x, cot, ext, up, down, left, right, acc):
    mid, chan = geo.mid, geo.chan
    taps = TAPS * TAPS
    shape = (geo.batch, geo.high, geo.wide, mid)
    lane = lax.broadcasted_iota(jnp.int32, (geo.batch, geo.ext, geo.wide, mid), 2)
    for kind in range(2):
        acc[...] = jnp.zeros_like(acc)
        for t in range(0, taps, 2):
            many = min(2, taps - t)
            if kind == 0:
                rhs = [k1s[(t + n) * chan : (t + n + 1) * chan, :] for n in range(many)]
                rhs = rhs[0] if many == 1 else jnp.concatenate(rhs, axis=1)
                y = jnp.dot(x[...], rhs, preferred_element_type=jnp.float32)
            else:
                rhs = k2s[t * mid : (t + many) * mid, :]
                y = lax.dot_general(
                    cot[...], rhs, (((1,), (1,)), ((), ())), preferred_element_type=jnp.float32
                )
            for n in range(many):
                a, e = divmod(t + n, TAPS)
                if kind == 0:
                    a, e = TAPS - 1 - a, TAPS - 1 - e
                acc[e, :, a : a + geo.high] += y[:, n * mid : (n + 1) * mid].reshape(shape)
        to_left = pltpu.roll(acc[0], geo.wide - 1, 2)
        to_right = pltpu.roll(acc[2], 1, 2)
        zero = jnp.zeros_like(to_left)
        main = (
            acc[1]
            + jnp.where(lane == geo.wide - 1, zero, to_left)
            + jnp.where(lane == 0, zero, to_right)
        )
        side = jnp.where(lane == geo.wide - 1, to_left, zero) + jnp.where(
            lane == 0, to_right, zero
        )
        base = kind * 2 * geo.plane
        ext[pl.ds(base, geo.plane), :] = main.reshape(geo.plane, mid)
        ext[pl.ds(base + geo.plane, geo.plane), :] = side.reshape(geo.plane, mid)
        for place, value in enumerate((main, side)):
            up[kind, place] = value[:, 0:2].astype(jnp.bfloat16)
            down[kind, place] = value[:, geo.high : geo.high + 2].astype(jnp.bfloat16)

        def column(place, j):
            return ext[pl.ds(base + place * geo.plane + j, geo.lines, stride=geo.wide), :]

        left[kind, 0] = column(1, geo.wide - 1)
        left[kind, 1] = column(0, 0)
        right[kind, 0] = column(0, geo.wide - 1)
        right[kind, 1] = column(1, 0)


def first_kernel(geo, pieces, *refs):
    if pieces:
        table, x, cot = refs[:3]
        ours, theirs = refs[3 : 3 + pieces], refs[3 + pieces : 3 + 2 * pieces]
        ext, up, down, left, right, k1s, acc, k2st, k2s, sems = refs[3 + 2 * pieces :]
        assemble(geo, table, ours, theirs, k1s, k2st, k2s, sems)
    else:
        x, cot, k1s, k2s, ext, up, down, left, right, acc = refs
    partial_convolutions(geo, k1s, k2s, x, cot, ext, up, down, left, right, acc)


def first_call(geo, x, cot, pieces=None, kernels=None):
    f32, bf16 = jnp.float32, jnp.bfloat16
    strip = (2, 2, geo.batch, 2, geo.wide, geo.mid)
    edge = (2, 2, geo.lines, geo.mid)
    outs = [
        jax.ShapeDtypeStruct((4 * geo.plane, geo.mid), f32),
        jax.ShapeDtypeStruct(strip, bf16),
        jax.ShapeDtypeStruct(strip, bf16),
        jax.ShapeDtypeStruct(edge, f32),
        jax.ShapeDtypeStruct(edge, f32),
    ]
    scratch = [pltpu.VMEM((TAPS, geo.batch, geo.ext, geo.wide, geo.mid), f32)]
    taps = TAPS * TAPS
    if pieces is not None:
        table, ours, theirs = pieces
        args = [table, x, cot, *ours, *theirs]
        specs = [pl.BlockSpec(memory_space=pltpu.SMEM), whole(x), whole(cot)]
        specs += [anywhere(p) for p in (*ours, *theirs)]
        outs.append(jax.ShapeDtypeStruct((taps * geo.chan, geo.mid), bf16))
        chips = geo.rows * geo.zs
        scratch += [
            pltpu.VMEM((chips, geo.unit, geo.mid), bf16),
            pltpu.VMEM((taps * geo.mid, geo.chan), bf16),
            pltpu.SemaphoreType.DMA((2 * chips,)),
        ]
        count = len(ours)
    else:
        args = [x, cot, *kernels]
        specs = [whole(p) for p in args]
        count = 0
    return pl.pallas_call(
        lambda *refs: first_kernel(geo, count, *refs),
        out_shape=outs,
        in_specs=specs,
        out_specs=[whole(o) for o in outs],
        scratch_shapes=scratch,
        compiler_params=pltpu.CompilerParams(vmem_limit_bytes=VMEM_LIMIT),
        cost_estimate=pl.CostEstimate(
            flops=4 * geo.pixels * taps * geo.chan * geo.mid,
            bytes_accessed=4 * taps * geo.chan * geo.mid + 4 * geo.pixels * geo.chan,
            transcendentals=0,
        ),
    )(*args)


def second_kernel(geo, place, k1_any, ext, above, below, lefts, rights, cot, out, k1s, full, shifted, lhs, sem):
    mid, chan, wide, high = geo.mid, geo.chan, geo.wide, geo.high
    load = pltpu.make_async_copy(k1_any, k1s, sem)
    load.start()
    full[...] = ext[...]
    f32 = jnp.float32
    for kind in range(2):
        for part in range(2):
            base = (kind * 2 + part) * geo.plane
            for b in range(geo.batch):
                top = base + b * geo.ext * wide
                two = (2 * wide, mid)
                full[pl.ds(top, 2 * wide), :] += above[kind, part, b].astype(f32).reshape(two)
                bottom = top + high * wide
                full[pl.ds(bottom, 2 * wide), :] += below[kind, part, b].astype(f32).reshape(two)
        base = kind * 2 * geo.plane

        def add(part, j, value):
            at = pl.ds(base + part * geo.plane + j, geo.lines, stride=wide)
            full[at, :] = full[at, :] + value.astype(f32)

        add(1, wide - 1, lefts[kind, 0])
        add(0, 0, lefts[kind, 1])
        add(0, wide - 1, rights[kind, 0])
        add(1, 0, rights[kind, 1])

    shape = (geo.batch, geo.ext, wide, mid)
    line = lax.broadcasted_iota(jnp.int32, shape, 1)
    lane = lax.broadcasted_iota(jnp.int32, shape, 2)
    row, col = place[0], place[1]
    inside = jnp.logical_and(
        jnp.logical_or(line > 0, row > 0),
        jnp.logical_or(line < geo.ext - 1, row < geo.rows - 1),
    )
    beside = jnp.logical_or(
        jnp.logical_and(lane == wide - 1, col > 0),
        jnp.logical_and(lane == 0, col < geo.cols - 1),
    )
    grads = []
    for part, keep in enumerate((inside, jnp.logical_and(inside, beside))):
        pre = full[pl.ds(part * geo.plane, geo.plane), :].reshape(shape)
        back = full[pl.ds((2 + part) * geo.plane, geo.plane), :].reshape(shape)
        s = jax.nn.sigmoid(pre)
        grad = back * (s * (1.0 + pre * (1.0 - s)))
        grad = jnp.where(keep, grad, jnp.zeros_like(grad))
        grads.append(grad.astype(jnp.bfloat16).astype(f32))
    main, side = grads
    shifted[0] = jnp.where(
        lane == wide - 1, pltpu.roll(side, wide - 1, 2), pltpu.roll(main, wide - 1, 2)
    )
    shifted[1] = main
    shifted[2] = jnp.where(lane == 0, pltpu.roll(side, 1, 2), pltpu.roll(main, 1, 2))
    taps = TAPS * TAPS
    for t in range(taps):
        a, e = divmod(t, TAPS)
        window = shifted[e, :, TAPS - 1 - a : TAPS - 1 - a + high]
        lhs[:, t * mid : (t + 1) * mid] = window.reshape(geo.pixels, mid).astype(jnp.bfloat16)
    load.wait()
    tile = 2 * mid
    for n in range(chan // tile):
        rhs = jnp.concatenate(
            [k1s[t * chan + n * tile : t * chan + (n + 1) * tile, :] for t in range(taps)], axis=1
        )
        y = lax.dot_general(
            lhs[...], rhs, (((1,), (1,)), ((), ())), preferred_element_type=f32
        )
        at = slice(n * tile, (n + 1) * tile)
        out[:, at] = (cot[:, at].astype(f32) + y).astype(jnp.bfloat16)


def second_call(geo, place, k1, ext, above, below, lefts, rights, cot):
    taps = TAPS * TAPS
    out = jax.ShapeDtypeStruct((geo.pixels, geo.chan), jnp.bfloat16)
    args = [place, k1, ext, above, below, lefts, rights, cot]
    specs = [pl.BlockSpec(memory_space=pltpu.SMEM), anywhere(k1)] + [whole(a) for a in args[2:]]
    return pl.pallas_call(
        lambda *refs: second_kernel(geo, *refs),
        out_shape=out,
        in_specs=specs,
        out_specs=whole(out),
        scratch_shapes=[
            pltpu.VMEM((taps * geo.chan, geo.mid), jnp.bfloat16),
            pltpu.VMEM((4 * geo.plane, geo.mid), jnp.float32),
            pltpu.VMEM((TAPS, geo.batch, geo.ext, geo.wide, geo.mid), jnp.float32),
            pltpu.VMEM((geo.pixels, taps * geo.mid), jnp.bfloat16),
            pltpu.SemaphoreType.DMA,
        ],
        compiler_params=pltpu.CompilerParams(vmem_limit_bytes=VMEM_LIMIT),
        cost_estimate=pl.CostEstimate(
            flops=2 * geo.pixels * taps * geo.chan * geo.mid,
            bytes_accessed=2 * taps * geo.chan * geo.mid + 4 * geo.pixels * geo.chan,
            transcendentals=geo.plane * geo.mid * 2,
        ),
    )(*args)


def shift(x, axis, forward):
    count = lax.axis_size(axis)
    pairs = [(i, i + 1) if forward else (i + 1, i) for i in range(count - 1)]
    return lax.ppermute(x, axis, pairs)


def edge_of(strip, parts_and_columns):
    return jnp.stack([strip[:, part, :, :, j] for part, j in parts_and_columns], axis=1)


def shards(inputs, cotangent, w_in, w_out):
    geo = Geometry(inputs, w_in)
    row, col = lax.axis_index("row"), lax.axis_index("col")
    core = col % 2
    x = inputs.reshape(geo.pixels, geo.chan)
    cot = cotangent.reshape(geo.pixels, geo.chan)
    if geo.pieces_fit():
        ours, theirs = gather_pieces(geo, w_in, w_out, core)
        ext, up, down, left, right, k1 = first_call(
            geo, x, cot, pieces=(chip_table(geo, core), ours, theirs)
        )
    else:
        k1 = lax.all_gather(w_in, AXES, axis=0, tiled=True).reshape(-1, geo.mid)
        k2 = lax.all_gather(w_out, AXES, axis=0, tiled=True).reshape(-1, geo.chan)
        ext, up, down, left, right = first_call(geo, x, cot, kernels=(k1, k2))
    above = shift(down, "row", True)
    below = shift(up, "row", False)
    last = geo.wide - 1
    edges = []
    for edge, where in ((left, ((1, last), (0, 0))), (right, ((0, last), (1, 0)))):
        full = edge.reshape(2, 2, geo.batch, geo.ext, geo.mid)
        top = edge_of(above, where).astype(jnp.float32)
        bottom = edge_of(below, where).astype(jnp.float32)
        gap = jnp.zeros((2, 2, geo.batch, geo.ext - 4, geo.mid), jnp.float32)
        full = full + jnp.concatenate([top, gap, bottom], axis=3)
        edges.append(full.astype(jnp.bfloat16).reshape(edge.shape))
    lefts = shift(edges[1], "col", True)
    rights = shift(edges[0], "col", False)
    place = jnp.stack([row, col]).astype(jnp.int32)
    out = second_call(geo, place, k1, ext, above, below, lefts, rights, cot)
    return out.reshape(inputs.shape)


def solution(mesh):
    return jax.shard_map(
        shards,
        mesh=mesh,
        in_specs=(
            P(None, "row", "col", None),
            P(None, "row", "col", None),
            P(("row", "col")),
            P(("row", "col")),
        ),
        out_specs=P(None, "row", "col", None),
        check_vma=False,
    )
```

```python
import jax
import jax.numpy as jnp
from jax import lax
from jax.experimental import pallas as pl
from jax.experimental.pallas import tpu as pltpu
from jax.sharding import PartitionSpec as P

AXES = ("row", "col")
VMEM_LIMIT = 16 * 1024 * 1024
TAPS = 3


def is_power(n):
    return n > 0 and n & (n - 1) == 0


def whole(array):
    return pl.BlockSpec(memory_space=pltpu.VMEM)


def far(array):
    return pl.BlockSpec(memory_space=pltpu.HBM)


class Geometry:
    def __init__(self, inputs, w_in):
        self.batch, self.high, self.wide, self.chan = inputs.shape
        self.rows, self.cols = lax.axis_size("row"), lax.axis_size("col")
        self.zs = self.cols // 2
        self.shard = w_in.shape[0]
        self.mid = self.shard * self.rows * self.cols // (TAPS * TAPS * self.chan)
        self.pixels = self.batch * self.high * self.wide
        self.ext = self.high + 2
        self.lines = self.batch * self.ext
        self.plane = self.lines * self.wide
        self.deep1 = self.shard // self.mid
        self.deep2 = self.shard // self.chan
        self.blocks = self.chan // self.mid

    def pieces_fit(self):
        return (
            self.cols % 2 == 0
            and is_power(self.zs)
            and is_power(self.rows)
            and self.rows >= 2
            and self.shard % self.chan == 0
            and self.chan % self.mid == 0
            and (2 * self.deep1) % 16 == 0
            and (4 * self.deep2) % 16 == 0
        )


def device_perm(geo, move):
    pairs = []
    for row in range(geo.rows):
        for col in range(geo.cols):
            r, z, k = move(row, col // 2, col % 2)
            pairs.append((row * geo.cols + col, r * geo.cols + z * 2 + k))
    return pairs


def send(x, perm):
    return lax.ppermute(x, AXES, perm)


def row_bits(geo, core):
    bits = [1 << i for i in range(geo.rows.bit_length() - 1)]
    return bits if core == 0 else bits[::-1]


def row_masks(geo, core):
    masks = [0]
    for bit in row_bits(geo, core):
        masks = masks + [m ^ bit for m in masks]
    return masks


def after(x, *others):
    return lax.optimization_barrier((x, *others))[0]


def double_rows(geo, x, step):
    perm = device_perm(geo, lambda r, z, k: (r ^ row_bits(geo, k)[step], z, k))
    return send(x, perm)


def row_stages(geo, parts, holds, split):
    held = parts
    steps = len(row_bits(geo, 0))
    for step in range(steps):
        held = held[0] if len(held) == 1 else jnp.concatenate(held, axis=0)
        if step < len(holds):
            held = after(held, *holds[step])
        if split and step == steps - 1:
            first, second = held[:, : geo.deep1], held[:, geo.deep1 :]
            return [held, double_rows(geo, first, step), double_rows(geo, second, step)]
        held = [held, double_rows(geo, held, step)]
    return held


def depth_groups(geo, own):
    found = {0: own}
    for i in reversed(range(geo.zs.bit_length() - 1)):
        perm = device_perm(geo, lambda r, z, k: (r, z ^ (1 << i), k))
        found.update({mask ^ (1 << i): send(x, perm) for mask, x in list(found.items())})
    masks = list(range(geo.zs))
    split = [masks[:1], masks[1:-1], masks[-1:]] if geo.zs > 1 else [masks]
    return [(group, [found[m] for m in group]) for group in split if group]


def gather_pieces(geo, w_in, w_out):
    k1 = w_in.reshape(1, geo.deep1, geo.mid)
    k2 = w_out.reshape(geo.deep2, geo.blocks, geo.mid).transpose(1, 0, 2)
    own = jnp.concatenate([k1, k2.reshape(1, geo.deep1, geo.mid)], axis=1)
    groups = depth_groups(geo, own)
    last = groups[-1][1][-1]
    done = []
    for n, (_, parts) in enumerate(groups):
        holds = []
        if n == 1 and len(groups) == 3:
            holds = [[done[0][0]], [last, done[0][1]]]
        if n == 2:
            holds = [[done[1][0]]]
        done.append(row_stages(geo, parts, holds, n == len(groups) - 1))
    return [(masks, arrays) for (masks, _), arrays in zip(groups, done)]


def swap_cores(geo, x):
    return send(x, device_perm(geo, lambda r, z, k: (r, z, 1 - k)))


def chip_table(geo, core, groups):
    row = lax.axis_index("row")
    z = lax.axis_index("col") // 2
    table = []
    for masks, _ in groups:
        depth = z ^ jnp.array(masks)[None, :]
        both = [
            ((row ^ jnp.array(row_masks(geo, k))[:, None]) * geo.zs + depth).reshape(-1)
            for k in (0, 1)
        ]
        table += [jnp.where(core == 0, *both), jnp.where(core == 0, *both[::-1])]
    return jnp.concatenate([jnp.asarray([core]), *table]).astype(jnp.int32)


def place_rows(target, base, offset, columns, rows):
    skew = offset % 16
    at = pl.multiple_of(base + (offset - skew), 16)
    if skew:
        rows = jnp.concatenate([target[pl.ds(at, 16), columns][:skew], rows], axis=0)
    target[pl.ds(at, rows.shape[0]), columns] = rows


def place_first(geo, chip, of_core, rows, k1s):
    base = pl.multiple_of(chip * (2 * geo.deep1), 16)
    place_rows(k1s, base, of_core * geo.deep1, slice(0, geo.mid), rows)


def place_second(geo, chip, of_core, rows, k2s):
    base = pl.multiple_of((chip // 2) * (4 * geo.deep2), 16)
    for odd in range(2):

        @pl.when(chip % 2 == odd)
        def _():
            for b in range(geo.blocks):
                columns = slice(b * geo.mid, (b + 1) * geo.mid)
                block = rows[b * geo.deep2 : (b + 1) * geo.deep2]
                offset = (2 * odd + of_core) * geo.deep2
                place_rows(k2s, base, offset, columns, block)


def place_array(geo, table, start, source, ref, k1s, k2s):
    core = table[0]

    @pl.loop(0, ref.shape[0])
    def _(n):
        chip = table[start + n]
        for of_core in range(2):

            @pl.when(core == (source ^ of_core))
            def _():
                if k1s is not None:
                    place_first(geo, chip, of_core, ref[n, : geo.deep1], k1s)
                if k2s is not None:
                    place_second(geo, chip, of_core, ref[n, ref.shape[1] - geo.deep1 :], k2s)


def weights_calls(geo, table, groups, x):
    start = 1
    weights, ext = [], None

    def pieces(starts, arrays, waits):
        theirs = [swap_cores(geo, after(y, *w) if w else y) for y, w in zip(arrays, waits)]
        return [
            (at + source * many, source, y)
            for source, ys in enumerate((arrays, theirs))
            for at, y in zip(starts, ys)
        ]

    held, first, second = groups[-1][1]
    for masks, arrays in groups[:-1]:
        many = geo.rows * len(masks)
        starts = [start, start + arrays[0].shape[0]]
        waits = [[], [*weights[:1], held]] if weights else [[], []]
        weights = early_call(geo, table, pieces(starts, arrays, waits), weights)
        start += 2 * many
    many = geo.rows * len(groups[-1][0])
    next_ = start + held.shape[0]
    wholes = pieces([start], [held], [[]])
    firsts = pieces([next_], [first], [weights[:1]])
    ext, *weights = first_call(geo, table, x, weights, (wholes, firsts))
    return ext, weights, pieces([next_], [second], [[ext]])


def weights_shapes(geo):
    taps = TAPS * TAPS
    return [
        jax.ShapeDtypeStruct((taps * geo.chan, geo.mid), jnp.bfloat16),
        jax.ShapeDtypeStruct((taps * geo.mid, geo.chan), jnp.bfloat16),
    ]


def smem():
    return pl.BlockSpec(memory_space=pltpu.SMEM)


def parameters():
    return pltpu.CompilerParams(vmem_limit_bytes=VMEM_LIMIT)


def early_call(geo, table, pieces, weights):
    def kernel(table, *refs):
        k1s, k2s = refs[-2:]
        for (start, source, _), ref in zip(pieces, refs):
            place_array(geo, table, start, source, ref, k1s, k2s)

    arrays = [x for _, _, x in pieces]
    outs = weights_shapes(geo)
    return pl.pallas_call(
        kernel,
        out_shape=outs,
        in_specs=[smem()] + [whole(x) for x in (*arrays, *weights)],
        out_specs=[whole(o) for o in outs],
        input_output_aliases={1 + len(arrays) + n: n for n in range(len(weights))},
        compiler_params=parameters(),
        cost_estimate=pl.CostEstimate(flops=0, bytes_accessed=0, transcendentals=0),
    )(table, *arrays, *weights)


def partial_convolution(geo, kind, weights, tile, ext, acc):
    mid, chan, wide, high = geo.mid, geo.chan, geo.wide, geo.high
    taps = TAPS * TAPS
    shape = (geo.batch, high, wide, mid)
    lane = lax.broadcasted_iota(jnp.int32, (geo.batch, geo.ext, wide, mid), 2)
    acc[...] = jnp.zeros_like(acc)
    for t in range(0, taps, 2):
        many = min(2, taps - t)
        if kind == 0:
            rhs = [weights[(t + n) * chan : (t + n + 1) * chan, :] for n in range(many)]
            rhs = rhs[0] if many == 1 else jnp.concatenate(rhs, axis=1)
            y = jnp.dot(tile[...], rhs, preferred_element_type=jnp.float32)
        else:
            rhs = weights[t * mid : (t + many) * mid, :]
            y = lax.dot_general(
                tile[...], rhs, (((1,), (1,)), ((), ())), preferred_element_type=jnp.float32
            )
        for n in range(many):
            a, e = divmod(t + n, TAPS)
            if kind == 0:
                a, e = TAPS - 1 - a, TAPS - 1 - e
            acc[e, :, a : a + high] += y[:, n * mid : (n + 1) * mid].reshape(shape)
    to_left = pltpu.roll(acc[0], wide - 1, 2)
    to_right = pltpu.roll(acc[2], 1, 2)
    zero = jnp.zeros_like(to_left)
    main = (
        acc[1]
        + jnp.where(lane == wide - 1, zero, to_left)
        + jnp.where(lane == 0, zero, to_right)
    )
    side = jnp.where(lane == wide - 1, to_left, zero) + jnp.where(lane == 0, to_right, zero)
    ext[pl.ds(0, geo.plane), :] = main.reshape(geo.plane, mid)
    ext[pl.ds(geo.plane, geo.plane), :] = side.reshape(geo.plane, mid)


def column(geo, ext, part, j):
    return ext[pl.ds(part * geo.plane + j, geo.lines, stride=geo.wide), :]


def first_call(geo, table, x, weights, pieces=None):
    ext = jax.ShapeDtypeStruct((2 * geo.plane, geo.mid), jnp.float32)
    wholes, firsts = pieces if pieces else ([], [])
    arrays = [x for _, _, x in wholes + firsts]
    count = len(arrays)

    def kernel(table, x, *refs):
        tile, acc, sem = refs[-3:]
        load = pltpu.make_async_copy(x, tile, sem)
        load.start()
        if pieces:
            ext, k1s, k2s = refs[-6:-3]
            for (start, source, _), ref in zip(wholes, refs):
                place_array(geo, table, start, source, ref, k1s, k2s)
            for (start, source, _), ref in zip(firsts, refs[len(wholes) :]):
                place_array(geo, table, start, source, ref, k1s, None)
        else:
            k1s, ext = refs[0], refs[-4]
        load.wait()
        partial_convolution(geo, 0, k1s, tile, ext, acc)

    args = [table, x, *arrays, *weights]
    outs = [ext] + (weights_shapes(geo) if pieces else [])
    return pl.pallas_call(
        kernel,
        out_shape=outs,
        in_specs=[smem(), far(x)] + [whole(a) for a in args[2:]],
        out_specs=[whole(o) for o in outs],
        scratch_shapes=[
            pltpu.VMEM(x.shape, x.dtype),
            pltpu.VMEM((TAPS, geo.batch, geo.ext, geo.wide, geo.mid), jnp.float32),
            pltpu.SemaphoreType.DMA,
        ],
        input_output_aliases={2 + count + n: 1 + n for n in range(len(weights))} if pieces else {},
        compiler_params=parameters(),
        cost_estimate=pl.CostEstimate(flops=0, bytes_accessed=0, transcendentals=0),
    )(*args)


def back_call(geo, table, cot, ext_pre, k2, pieces=None):
    ext = jax.ShapeDtypeStruct((2 * geo.plane, geo.mid), jnp.float32)
    edge = jax.ShapeDtypeStruct((2, 2, geo.lines, geo.mid), jnp.bfloat16)
    pieces = pieces or []
    arrays = [x for _, _, x in pieces]
    count = len(arrays)

    def kernel(table, cot, ext_pre, *refs):
        k2_in = refs[count]
        ext, inner, outer = refs[count + 1 : count + 4]
        tile, acc, sem = refs[-3:]
        load = pltpu.make_async_copy(cot, tile, sem)
        load.start()
        k2s = refs[-4] if count else k2_in
        for (start, source, _), ref in zip(pieces, refs):
            place_array(geo, table, start, source, ref, None, k2s)
        load.wait()
        partial_convolution(geo, 1, k2s, tile, ext, acc)
        left, right = ((1, geo.wide - 1), (0, 0)), ((0, geo.wide - 1), (1, 0))
        core = table[0]
        for out, is_right in ((inner, core == 0), (outer, core != 0)):
            for kind, plane in enumerate((ext_pre, ext)):
                for n in range(2):
                    value = jnp.where(
                        is_right, column(geo, plane, *right[n]), column(geo, plane, *left[n])
                    )
                    out[kind, n] = value.astype(jnp.bfloat16)

    args = [table, cot, ext_pre, *arrays, k2]
    outs = [ext, edge, edge] + (weights_shapes(geo)[1:] if count else [])
    return pl.pallas_call(
        kernel,
        out_shape=outs,
        in_specs=[smem(), far(cot)] + [whole(a) for a in args[2:]],
        out_specs=[whole(o) for o in outs],
        scratch_shapes=[
            pltpu.VMEM(cot.shape, cot.dtype),
            pltpu.VMEM((TAPS, geo.batch, geo.ext, geo.wide, geo.mid), jnp.float32),
            pltpu.SemaphoreType.DMA,
        ],
        input_output_aliases={3 + count: 3} if count else {},
        compiler_params=parameters(),
        cost_estimate=pl.CostEstimate(
            flops=2 * geo.pixels * TAPS * TAPS * geo.chan * geo.mid,
            bytes_accessed=2 * TAPS * TAPS * geo.chan * geo.mid,
            transcendentals=0,
        ),
    )(*args)[:3]


def beside(geo, inner, outer):
    swap = device_perm(geo, lambda r, z, k: (r, z, 1 - k))
    pairs = []
    for row in range(geo.rows):
        for col in range(1, geo.cols - 1, 2):
            a, b = row * geo.cols + col, row * geo.cols + col + 1
            pairs += [(a, b), (b, a)]
    return send(inner, swap), send(outer, pairs)


def join_call(geo, place, ext_pre, ext_back, inner, outer):
    full = jax.ShapeDtypeStruct((4 * geo.plane, geo.mid), jnp.float32)
    strip = jax.ShapeDtypeStruct((2, 2, geo.batch, 2 * geo.wide, geo.mid), jnp.bfloat16)

    def kernel(place, ext_pre, ext_back, inner, outer, full, near_strip, next_strip):
        core = place[0]
        even = place[1] % 2 == 0
        wide = geo.wide
        for kind, ext in enumerate((ext_pre, ext_back)):
            base = kind * 2 * geo.plane
            full[pl.ds(base, 2 * geo.plane), :] = ext[...]

            def add(part, j, value):
                at = pl.ds(base + part * geo.plane + j, geo.lines, stride=wide)
                full[at, :] = full[at, :] + value

            near = [inner[kind, n].astype(jnp.float32) for n in range(2)]
            next_ = [outer[kind, n].astype(jnp.float32) for n in range(2)]
            left = [jnp.where(core == 0, b, a) for a, b in zip(near, next_)]
            right = [jnp.where(core == 0, a, b) for a, b in zip(near, next_)]
            add(1, wide - 1, left[0])
            add(0, 0, left[1])
            add(0, wide - 1, right[0])
            add(1, 0, right[1])
            for part in range(2):
                for b in range(geo.batch):
                    top = base + part * geo.plane + b * geo.ext * wide
                    for out, low in ((near_strip, even), (next_strip, jnp.logical_not(even))):
                        line = pl.multiple_of(top + jnp.where(low, geo.high * wide, 0), 8)
                        two = full[pl.ds(line, 2 * wide), :]
                        out[kind, part, b] = two.astype(jnp.bfloat16)

    args = [place, ext_pre, ext_back, inner, outer]
    return pl.pallas_call(
        kernel,
        out_shape=[full, strip, strip],
        in_specs=[smem()] + [whole(a) for a in args[1:]],
        out_specs=[whole(o) for o in (full, strip, strip)],
        compiler_params=parameters(),
    )(*args)


def gradient(geo, place, full, lines, shifted):
    mid, wide = geo.mid, geo.wide
    f32 = jnp.float32
    first, count = lines
    shape = (geo.batch, count, wide, mid)
    line = lax.broadcasted_iota(jnp.int32, shape, 1) + first
    lane = lax.broadcasted_iota(jnp.int32, shape, 2)
    row, col = place[1], place[2]
    inside = jnp.logical_and(
        jnp.logical_or(line > 0, row > 0),
        jnp.logical_or(line < geo.ext - 1, row < geo.rows - 1),
    )
    beside = jnp.logical_or(
        jnp.logical_and(lane == wide - 1, col > 0),
        jnp.logical_and(lane == 0, col < geo.cols - 1),
    )
    grads = []
    for part, keep in enumerate((inside, jnp.logical_and(inside, beside))):
        pre, back = full(0, part), full(1, part)
        s = jax.nn.sigmoid(pre)
        grad = back * (s * (1.0 + pre * (1.0 - s)))
        grad = jnp.where(keep, grad, jnp.zeros_like(grad))
        grads.append(grad.astype(jnp.bfloat16).astype(f32))
    main, side = grads
    left = jnp.where(
        lane == wide - 1, pltpu.roll(side, wide - 1, 2), pltpu.roll(main, wide - 1, 2)
    )
    right = jnp.where(lane == 0, pltpu.roll(side, 1, 2), pltpu.roll(main, 1, 2))
    for e, value in enumerate((left, main, right)):
        shifted[e, :, first : first + count] = value


def windows(geo, shifted, spans, lhs):
    for t in range(TAPS * TAPS):
        a, e = divmod(t, TAPS)
        parts = []
        for first, count in spans:
            at = first + TAPS - 1 - a
            parts.append(shifted[e, :, at : at + count])
        window = parts[0] if len(parts) == 1 else jnp.concatenate(parts, axis=1)
        window = window.reshape(-1, geo.mid).astype(jnp.bfloat16)
        lhs[:, t * geo.mid : (t + 1) * geo.mid] = window


def convolve_back(geo, lhs, k1s, cot, spans, out, tiles, sems):
    width = 2 * geo.mid
    at = [sum(many for _, many in spans[:n]) for n in range(len(spans))]
    loads, stores = [], []
    for n, (start, many) in enumerate(spans):
        here, there = pl.ds(at[n], many), pl.ds(start, many)
        loads.append(
            pltpu.make_async_copy(cot.at[:, there], tiles.at[:, here], sems.at[0, n])
        )
        stores.append(
            pltpu.make_async_copy(tiles.at[:, here], out.at[:, there], sems.at[1, n])
        )
    for load in loads:
        load.start()
    yield
    for load in loads:
        load.wait()
    for n in range(geo.chan // width):
        columns = slice(n * width, (n + 1) * width)
        rhs = jnp.concatenate(
            [
                k1s[t * geo.chan + n * width : t * geo.chan + (n + 1) * width, :]
                for t in range(TAPS * TAPS)
            ],
            axis=1,
        )
        y = lax.dot_general(
            lhs[...], rhs, (((1,), (1,)), ((), ())), preferred_element_type=jnp.float32
        )
        y = y.reshape(geo.batch, -1, width)
        tiles[:, :, columns] = (tiles[:, :, columns].astype(jnp.float32) + y).astype(jnp.bfloat16)
    for store in stores:
        store.start()
    for store in stores:
        store.wait()
    yield


def inner_kernel(geo, place, k1s, ext, cot, out, shifted, lhs, tiles, sems):
    wide, mid, high = geo.wide, geo.mid, geo.high
    steps = convolve_back(
        geo, lhs, k1s, cot, [(2 * wide, (high - 4) * wide)], out, tiles, sems
    )
    next(steps)
    count = geo.ext - 4

    def full(kind, part):
        base = (kind * 2 + part) * geo.plane
        plane = ext[pl.ds(base, geo.plane), :].reshape(geo.batch, geo.ext, wide, mid)
        return plane[:, 2 : 2 + count]

    gradient(geo, place, full, (2, count), shifted)
    windows(geo, shifted, [(2, high - 4)], lhs)
    next(steps)


def outer_kernel(geo, place, k1s, ext, near_strip, next_strip, cot, given, out, shifted, lhs, tiles, sems):
    wide, mid, high = geo.wide, geo.mid, geo.high
    two = (geo.batch, 2, wide, mid)
    steps = convolve_back(
        geo, lhs, k1s, cot, [(0, 2 * wide), ((high - 2) * wide, 2 * wide)], out, tiles, sems
    )
    next(steps)
    even = place[1] % 2 == 0
    for first in (0, geo.ext - 4):
        near = jnp.logical_xor(even, first == 0)

        def full(kind, part):
            base = (kind * 2 + part) * geo.plane
            plane = ext[pl.ds(base, geo.plane), :].reshape(geo.batch, geo.ext, wide, mid)
            plane = plane[:, first : first + 4]
            got = jnp.where(
                near,
                near_strip[kind, part].astype(jnp.float32),
                next_strip[kind, part].astype(jnp.float32),
            ).reshape(two)
            none = jnp.zeros_like(got)
            return plane + jnp.concatenate([none, got] if first else [got, none], axis=1)

        gradient(geo, place, full, (first, 4), shifted)
    windows(geo, shifted, [(0, 2), (high - 2, 2)], lhs)
    next(steps)


def second_calls(geo, place, k1, ext, near_strip, next_strip, cot):
    taps = TAPS * TAPS
    image = (geo.batch, geo.high * geo.wide, geo.chan)
    out = jax.ShapeDtypeStruct(image, jnp.bfloat16)
    cot = cot.reshape(image)

    def call(kernel, args, rows, given):
        pixels = rows * geo.wide
        return pl.pallas_call(
            lambda *refs: kernel(geo, *refs),
            out_shape=out,
            in_specs=[smem()] + [whole(a) for a in args[1:]] + [far(a) for a in (cot, *given)],
            out_specs=far(out),
            scratch_shapes=[
                pltpu.VMEM((TAPS, geo.batch, geo.ext, geo.wide, geo.mid), jnp.float32),
                pltpu.VMEM((geo.batch * pixels, taps * geo.mid), jnp.bfloat16),
                pltpu.VMEM((geo.batch, pixels, geo.chan), jnp.bfloat16),
                pltpu.SemaphoreType.DMA((2, 2)),
            ],
            input_output_aliases={len(args) + 1: 0} if given else {},
            compiler_params=pltpu.CompilerParams(vmem_limit_bytes=VMEM_LIMIT),
            cost_estimate=pl.CostEstimate(
                flops=2 * geo.batch * pixels * taps * geo.chan * geo.mid,
                bytes_accessed=2 * taps * geo.chan * geo.mid,
                transcendentals=geo.plane * geo.mid,
            ),
        )(*args, cot, *given)

    inner = call(inner_kernel, [place, k1, ext], geo.high - 4, [])
    return call(outer_kernel, [place, k1, ext, near_strip, next_strip], 4, [inner])


def along_rows(geo, near_strip, next_strip):
    pair = [(i, i ^ 1) for i in range(geo.rows) if i ^ 1 < geo.rows]
    between = [p for i in range(1, geo.rows - 1, 2) for p in ((i, i + 1), (i + 1, i))]
    return lax.ppermute(near_strip, "row", pair), lax.ppermute(next_strip, "row", between)


def shards(inputs, cotangent, w_in, w_out):
    geo = Geometry(inputs, w_in)
    row, col = lax.axis_index("row"), lax.axis_index("col")
    core = col % 2
    x = inputs.reshape(geo.pixels, geo.chan)
    cot = cotangent.reshape(geo.pixels, geo.chan)
    place = jnp.stack([core, row, col]).astype(jnp.int32)
    if geo.pieces_fit():
        groups = gather_pieces(geo, w_in, w_out)
        table = chip_table(geo, core, groups)
        ext_pre, (k1, k2), pieces = weights_calls(geo, table, groups, x)
        ext_back, inner, outer = back_call(geo, table, cot, ext_pre, k2, pieces)
    else:
        k1 = lax.all_gather(w_in, AXES, axis=0, tiled=True).reshape(-1, geo.mid)
        k2 = lax.all_gather(w_out, AXES, axis=0, tiled=True).reshape(-1, geo.chan)
        (ext_pre,) = first_call(geo, place, x, [k1])
        ext_back, inner, outer = back_call(geo, place, cot, ext_pre, k2)
    inner, outer = beside(geo, inner, outer)
    full, *strips = join_call(geo, place, ext_pre, ext_back, inner, outer)
    out = second_calls(geo, place, k1, full, *along_rows(geo, *strips), cot)
    return out.reshape(inputs.shape)


def solution(mesh):
    return jax.shard_map(
        shards,
        mesh=mesh,
        in_specs=(
            P(None, "row", "col", None),
            P(None, "row", "col", None),
            P(("row", "col")),
            P(("row", "col")),
        ),
        out_specs=P(None, "row", "col", None),
        check_vma=False,
    )
```

```python
import jax
import jax.numpy as jnp
from jax import lax
from jax.experimental import pallas as pl
from jax.experimental.pallas import tpu as pltpu
from jax.sharding import PartitionSpec as P

AXES = ("row", "col")
VMEM_LIMIT = 16 * 1024 * 1024
TAPS = 3
PLAN = {
    "far_half": True,
    "modes": {"c": "cat", "d": "sep", "o": "cat"},
    "holds": {},
    "early": ("o", "c", "d"),
    "pin": True,
    "late": 1,
    "late_c": 1,
    "table": "d2",
    "costs": (0, 0),
}


def is_power(n):
    return n > 0 and n & (n - 1) == 0


def whole(array):
    return pl.BlockSpec(memory_space=pltpu.VMEM)


def far(array):
    return pl.BlockSpec(memory_space=pltpu.HBM)


class Geometry:
    def __init__(self, inputs, w_in):
        self.batch, self.high, self.wide, self.chan = inputs.shape
        self.rows, self.cols = lax.axis_size("row"), lax.axis_size("col")
        self.zs = self.cols // 2
        self.shard = w_in.shape[0]
        self.mid = self.shard * self.rows * self.cols // (TAPS * TAPS * self.chan)
        self.pixels = self.batch * self.high * self.wide
        self.ext = self.high + 2
        self.lines = self.batch * self.ext
        self.plane = self.lines * self.wide
        self.deep1 = self.shard // self.mid
        self.deep2 = self.shard // self.chan
        self.blocks = self.chan // self.mid

    def pieces_fit(self):
        return (
            self.cols % 2 == 0
            and is_power(self.zs)
            and is_power(self.rows)
            and self.rows >= 2
            and self.shard % self.chan == 0
            and self.chan % self.mid == 0
            and (2 * self.deep1) % 16 == 0
            and (4 * self.deep2) % 16 == 0
        )


def device_perm(geo, move):
    pairs = []
    for row in range(geo.rows):
        for col in range(geo.cols):
            r, z, k = move(row, col // 2, col % 2)
            pairs.append((row * geo.cols + col, r * geo.cols + z * 2 + k))
    return pairs


def send(x, perm):
    return lax.ppermute(x, AXES, perm)


def row_bits(geo, core):
    bits = [1 << i for i in range(geo.rows.bit_length() - 1)]
    return bits if core == 0 else bits[::-1]


def row_masks(geo, core):
    masks = [0]
    for bit in row_bits(geo, core):
        masks = masks + [m ^ bit for m in masks]
    return masks


def after(x, *others):
    return lax.optimization_barrier((x, *others))[0]


def double_rows(geo, x, step):
    perm = device_perm(geo, lambda r, z, k: (r ^ row_bits(geo, k)[step], z, k))
    return send(x, perm)


def depth_groups(geo):
    masks = list(range(geo.zs))
    cut = max(1, geo.zs // 2 if PLAN["far_half"] else geo.zs - 1)
    groups = {"o": masks[:1], "c": masks[1:cut], "d": masks[cut:]}
    return {name: group for name, group in groups.items() if group}


def own_part(geo, w_in, w_out):
    def kernel(first, second, out):
        out[0, : geo.deep1] = first[...]
        target = lax.broadcasted_iota(jnp.int32, (geo.deep1, 1), 0)
        block = sum((target >= b * geo.deep2).astype(jnp.int32) for b in range(1, geo.blocks))
        wanted = (target - geo.deep2 * block) * geo.blocks + block
        source = lax.broadcasted_iota(jnp.int32, (geo.deep1, geo.deep1), 1)
        pick = (source == wanted).astype(jnp.bfloat16)
        rows = jnp.dot(pick, second[...], preferred_element_type=jnp.float32)
        out[0, geo.deep1 :] = rows.astype(jnp.bfloat16)

    out = jax.ShapeDtypeStruct((1, 2 * geo.deep1, geo.mid), jnp.bfloat16)
    args = [w.reshape(geo.deep1, geo.mid) for w in (w_in, w_out)]
    return pl.pallas_call(
        kernel,
        out_shape=out,
        in_specs=[whole(a) for a in args],
        out_specs=whole(out),
        compiler_params=parameters(),
    )(*args)


def gather_pieces(geo, w_in, w_out):
    own = own_part(geo, w_in, w_out)
    steps = len(row_bits(geo, 0))
    found = {"z0": own}

    def ready(name, x):
        held = [found[other] for other in PLAN["holds"].get(name, ()) if other in found]
        return after(x, *held) if held else x

    def along_z(mask):
        bit = mask & -mask
        perm = device_perm(geo, lambda r, z, k: (r, z ^ bit, k))
        name = f"z{mask}"
        found[name] = send(ready(name, found[f"z{mask ^ bit}"]), perm)

    def along_rows_of(name, x):
        parts, count = [x], 0
        for step in range(steps):
            if PLAN["modes"][name] == "cat":
                parts = [parts[0] if step == 0 else jnp.concatenate(parts, axis=0)]
            new = []
            for part in parts:
                key = f"{name}{count}"
                found[key] = double_rows(geo, ready(key, part), step)
                new.append(found[key])
                count += 1
            parts = parts + new
        return parts

    groups = depth_groups(geo)
    if geo.zs > 1:
        along_z(geo.zs // 2)
    done = {"o": along_rows_of("o", own)}
    for mask in sorted(range(1, geo.zs), key=lambda m: (m.bit_count(), m)):
        if mask != geo.zs // 2:
            along_z(mask)
    for name in groups:
        if name != "o":
            parts = [found[f"z{mask}"] for mask in groups[name]]
            x = parts[0] if len(parts) == 1 else jnp.concatenate(parts, axis=0)
            done[name] = along_rows_of(name, x)
    return done, found


def swap_cores(geo, x):
    return send(x, device_perm(geo, lambda r, z, k: (r, z, 1 - k)))


def chip_table(geo, core):
    row = lax.axis_index("row")
    z = lax.axis_index("col") // 2
    table = []
    for group in depth_groups(geo).values():
        depth = z ^ jnp.array(group)[None, :]
        both = [
            ((row ^ jnp.array(row_masks(geo, k))[:, None]) * geo.zs + depth).reshape(-1)
            for k in (0, 1)
        ]
        table += [jnp.where(core == 0, *both), jnp.where(core == 0, *both[::-1])]
    return jnp.concatenate([jnp.asarray([core]), *table]).astype(jnp.int32)


def place_rows(target, base, offset, columns, rows):
    skew = offset % 16
    at = pl.multiple_of(base + (offset - skew), 16)
    if skew:
        rows = jnp.concatenate([target[pl.ds(at, 16), columns][:skew], rows], axis=0)
    target[pl.ds(at, rows.shape[0]), columns] = rows


def place_first(geo, chip, of_core, rows, k1s):
    base = pl.multiple_of(chip * (2 * geo.deep1), 16)
    place_rows(k1s, base, of_core * geo.deep1, slice(0, geo.mid), rows)


def place_second(geo, chip, of_core, rows, k2s):
    base = pl.multiple_of((chip // 2) * (4 * geo.deep2), 16)
    for odd in range(2):

        @pl.when(chip % 2 == odd)
        def _():
            for b in range(geo.blocks):
                columns = slice(b * geo.mid, (b + 1) * geo.mid)
                block = rows[b * geo.deep2 : (b + 1) * geo.deep2]
                offset = (2 * odd + of_core) * geo.deep2
                place_rows(k2s, base, offset, columns, block)


def place_array(geo, table, start, source, ref, k1s, k2s):
    core = table[0]

    @pl.loop(0, ref.shape[0])
    def _(n):
        chip = table[start + n]
        for of_core in range(2):

            @pl.when(core == (source ^ of_core))
            def _():
                if k1s is not None:
                    place_first(geo, chip, of_core, ref[n, : geo.deep1], k1s)
                if k2s is not None:
                    place_second(geo, chip, of_core, ref[n, ref.shape[1] - geo.deep1 :], k2s)


def weights_calls(geo, table, groups, found, tiles):
    start = 1
    entries = {}
    last = list(groups)[-1]
    for name, arrays in groups.items():
        total = sum(y.shape[0] for y in arrays)
        at = start
        entries[name] = []
        for y in arrays:
            entries[name].append((at, total, y))
            at += y.shape[0]
        start += 2 * total

    def both(some, wait):
        theirs = [
            swap_cores(geo, after(y, wait) if wait is not None and n == len(some) - 1 else y)
            for n, (_, _, y) in enumerate(some)
        ]
        return [(at, 0, y) for at, _, y in some] + [
            (at + total, 1, y) for (at, total, _), y in zip(some, theirs)
        ]

    final = groups[last][-1]
    late = entries[last][-PLAN["late"] :]
    entries[last] = entries[last][: -PLAN["late"]]
    before = []
    if PLAN["late_c"] and len(groups) == 3:
        before = entries["c"][-1:]
        entries["c"] = entries["c"][:-1]
    weights = []
    for names in PLAN["early"]:
        pieces = []
        is_last = names == PLAN["early"][-1]
        loads = tiles if is_last else ()
        here = after(table, found[PLAN["table"]]) if is_last and PLAN["table"] in found else table
        for name in names:
            if entries.get(name):
                pieces += both(entries[name], weights[0] if weights and PLAN["pin"] else None)
        if pieces:
            weights = early_call(geo, here, pieces, weights[:2], loads)
    return weights[:2], weights[2:], both(before, final) + both(late, None)


def weights_shapes(geo):
    taps = TAPS * TAPS
    return [
        jax.ShapeDtypeStruct((taps * geo.chan, geo.mid), jnp.bfloat16),
        jax.ShapeDtypeStruct((taps * geo.mid, geo.chan), jnp.bfloat16),
    ]


def smem():
    return pl.BlockSpec(memory_space=pltpu.SMEM)


def parameters():
    return pltpu.CompilerParams(vmem_limit_bytes=VMEM_LIMIT)


def early_call(geo, table, pieces, weights, tiles=()):
    arrays = [x for _, _, x in pieces]
    count = len(arrays) + len(weights)

    def kernel(table, *refs):
        sem = refs[-1]
        outs = refs[count + len(tiles) : -1]
        loads = [
            pltpu.make_async_copy(refs[count + n], outs[2 + n], sem.at[n])
            for n in range(len(tiles))
        ]
        for load in loads:
            load.start()
        for (start, source, _), ref in zip(pieces, refs):
            place_array(geo, table, start, source, ref, *outs[:2])
        for load in loads:
            load.wait()

    outs = weights_shapes(geo) + [jax.ShapeDtypeStruct(t.shape, t.dtype) for t in tiles]
    return pl.pallas_call(
        kernel,
        out_shape=outs,
        in_specs=[smem()] + [whole(x) for x in (*arrays, *weights)] + [far(t) for t in tiles],
        out_specs=[whole(o) for o in outs],
        scratch_shapes=[pltpu.SemaphoreType.DMA((2,))],
        input_output_aliases={1 + len(arrays) + n: n for n in range(len(weights))},
        compiler_params=parameters(),
        cost_estimate=pl.CostEstimate(
            flops=0,
            bytes_accessed=PLAN["costs"][0] * 8 * TAPS * TAPS * geo.chan * geo.mid,
            transcendentals=0,
        ),
    )(table, *arrays, *weights, *tiles)


def partial_convolution(geo, kind, weights, tile, ext, acc):
    mid, chan, wide, high = geo.mid, geo.chan, geo.wide, geo.high
    taps = TAPS * TAPS
    shape = (geo.batch, high, wide, mid)
    lane = lax.broadcasted_iota(jnp.int32, (geo.batch, geo.ext, wide, mid), 2)
    acc[...] = jnp.zeros_like(acc)
    for t in range(0, taps, 2):
        many = min(2, taps - t)
        if kind == 0:
            rhs = [weights[(t + n) * chan : (t + n + 1) * chan, :] for n in range(many)]
            rhs = rhs[0] if many == 1 else jnp.concatenate(rhs, axis=1)
            y = jnp.dot(tile[...], rhs, preferred_element_type=jnp.float32)
        else:
            rhs = weights[t * mid : (t + many) * mid, :]
            y = lax.dot_general(
                tile[...], rhs, (((1,), (1,)), ((), ())), preferred_element_type=jnp.float32
            )
        for n in range(many):
            a, e = divmod(t + n, TAPS)
            if kind == 0:
                a, e = TAPS - 1 - a, TAPS - 1 - e
            acc[e, :, a : a + high] += y[:, n * mid : (n + 1) * mid].reshape(shape)
    to_left = pltpu.roll(acc[0], wide - 1, 2)
    to_right = pltpu.roll(acc[2], 1, 2)
    zero = jnp.zeros_like(to_left)
    main = (
        acc[1]
        + jnp.where(lane == wide - 1, zero, to_left)
        + jnp.where(lane == 0, zero, to_right)
    )
    side = jnp.where(lane == wide - 1, to_left, zero) + jnp.where(lane == 0, to_right, zero)
    ext[pl.ds(0, geo.plane), :] = main.reshape(geo.plane, mid)
    ext[pl.ds(geo.plane, geo.plane), :] = side.reshape(geo.plane, mid)


def column(geo, ext, part, j):
    return ext[pl.ds(part * geo.plane + j, geo.lines, stride=geo.wide), :]


def partial_call(geo, table, x, cot, weights, pieces=()):
    ext = jax.ShapeDtypeStruct((4 * geo.plane, geo.mid), jnp.float32)
    edge = jax.ShapeDtypeStruct((2, 2, geo.lines, geo.mid), jnp.bfloat16)
    arrays = [y for _, _, y in pieces]
    count = len(arrays)

    def kernel(table, x, cot, *refs):
        acc = refs[-1]
        outs = refs[count + len(weights) : -1]
        exts = [outs[0].at[pl.ds(kind * 2 * geo.plane, 2 * geo.plane)] for kind in range(2)]
        edges = outs[1:3]
        placed = outs[3:] if pieces else refs[:2]
        for (start, source, _), ref in zip(pieces, refs):
            place_array(geo, table, start, source, ref, *placed)
        for kind in range(2):
            partial_convolution(geo, kind, placed[kind], (x, cot)[kind], exts[kind], acc)
        left, right = ((1, geo.wide - 1), (0, 0)), ((0, geo.wide - 1), (1, 0))
        core = table[0]
        for out, is_right in zip(edges, (core == 0, core != 0)):
            for kind, plane in enumerate(exts):
                for n in range(2):
                    value = jnp.where(
                        is_right, column(geo, plane, *right[n]), column(geo, plane, *left[n])
                    )
                    out[kind, n] = value.astype(jnp.bfloat16)

    args = [table, x, cot, *arrays, *weights]
    outs = [ext, edge, edge] + (weights_shapes(geo) if pieces else [])
    alias = {3 + count + n: 3 + n for n in range(len(weights))}
    return pl.pallas_call(
        kernel,
        out_shape=outs,
        in_specs=[smem()] + [whole(a) for a in args[1:]],
        out_specs=[whole(o) for o in outs],
        scratch_shapes=[pltpu.VMEM((TAPS, geo.batch, geo.ext, geo.wide, geo.mid), jnp.float32)],
        input_output_aliases=alias if pieces else {},
        compiler_params=parameters(),
        cost_estimate=pl.CostEstimate(
            flops=PLAN["costs"][1] * 4 * geo.pixels * TAPS * TAPS * geo.chan * geo.mid,
            bytes_accessed=PLAN["costs"][1] * 4 * TAPS * TAPS * geo.chan * geo.mid,
            transcendentals=0,
        ),
    )(*args)


def beside(geo, inner, outer):
    swap = device_perm(geo, lambda r, z, k: (r, z, 1 - k))
    pairs = []
    for row in range(geo.rows):
        for col in range(1, geo.cols - 1, 2):
            a, b = row * geo.cols + col, row * geo.cols + col + 1
            pairs += [(a, b), (b, a)]
    return send(inner, swap), send(outer, pairs)


def join_call(geo, place, ext, inner, outer):
    full = jax.ShapeDtypeStruct((4 * geo.plane, geo.mid), jnp.float32)
    strip = jax.ShapeDtypeStruct((2, 2, geo.batch, 2 * geo.wide, geo.mid), jnp.bfloat16)

    def kernel(place, ext, inner, outer, full, near_strip, next_strip):
        core = place[0]
        even = place[1] % 2 == 0
        wide = geo.wide
        for kind in range(2):
            base = kind * 2 * geo.plane

            def add(part, j, value):
                at = pl.ds(base + part * geo.plane + j, geo.lines, stride=wide)
                full[at, :] = full[at, :] + value

            near = [inner[kind, n].astype(jnp.float32) for n in range(2)]
            next_ = [outer[kind, n].astype(jnp.float32) for n in range(2)]
            left = [jnp.where(core == 0, b, a) for a, b in zip(near, next_)]
            right = [jnp.where(core == 0, a, b) for a, b in zip(near, next_)]
            add(1, wide - 1, left[0])
            add(0, 0, left[1])
            add(0, wide - 1, right[0])
            add(1, 0, right[1])
            for part in range(2):
                for b in range(geo.batch):
                    top = base + part * geo.plane + b * geo.ext * wide
                    for out, low in ((near_strip, even), (next_strip, jnp.logical_not(even))):
                        line = pl.multiple_of(top + jnp.where(low, geo.high * wide, 0), 8)
                        two = full[pl.ds(line, 2 * wide), :]
                        out[kind, part, b] = two.astype(jnp.bfloat16)

    args = [place, ext, inner, outer]
    return pl.pallas_call(
        kernel,
        out_shape=[full, strip, strip],
        in_specs=[smem()] + [whole(a) for a in args[1:]],
        out_specs=[whole(o) for o in (full, strip, strip)],
        input_output_aliases={1: 0},
        compiler_params=parameters(),
    )(*args)


def gradient(geo, place, full, lines, shifted):
    mid, wide = geo.mid, geo.wide
    f32 = jnp.float32
    first, count = lines
    shape = (geo.batch, count, wide, mid)
    line = lax.broadcasted_iota(jnp.int32, shape, 1) + first
    lane = lax.broadcasted_iota(jnp.int32, shape, 2)
    row, col = place[1], place[2]
    inside = jnp.logical_and(
        jnp.logical_or(line > 0, row > 0),
        jnp.logical_or(line < geo.ext - 1, row < geo.rows - 1),
    )
    beside = jnp.logical_or(
        jnp.logical_and(lane == wide - 1, col > 0),
        jnp.logical_and(lane == 0, col < geo.cols - 1),
    )
    grads = []
    for part, keep in enumerate((inside, jnp.logical_and(inside, beside))):
        pre, back = full(0, part), full(1, part)
        s = jax.nn.sigmoid(pre)
        grad = back * (s * (1.0 + pre * (1.0 - s)))
        grad = jnp.where(keep, grad, jnp.zeros_like(grad))
        grads.append(grad.astype(jnp.bfloat16).astype(f32))
    main, side = grads
    left = jnp.where(
        lane == wide - 1, pltpu.roll(side, wide - 1, 2), pltpu.roll(main, wide - 1, 2)
    )
    right = jnp.where(lane == 0, pltpu.roll(side, 1, 2), pltpu.roll(main, 1, 2))
    for e, value in enumerate((left, main, right)):
        shifted[e, :, first : first + count] = value


def windows(geo, shifted, spans, lhs):
    for t in range(TAPS * TAPS):
        a, e = divmod(t, TAPS)
        parts = []
        for first, count in spans:
            at = first + TAPS - 1 - a
            parts.append(shifted[e, :, at : at + count])
        window = parts[0] if len(parts) == 1 else jnp.concatenate(parts, axis=1)
        window = window.reshape(-1, geo.mid).astype(jnp.bfloat16)
        lhs[:, t * geo.mid : (t + 1) * geo.mid] = window


def convolve_back(geo, lhs, k1s, cot, spans, out, tiles, sems):
    width = 2 * geo.mid
    for n in range(geo.chan // width):
        columns = slice(n * width, (n + 1) * width)
        rhs = jnp.concatenate(
            [
                k1s[t * geo.chan + n * width : t * geo.chan + (n + 1) * width, :]
                for t in range(TAPS * TAPS)
            ],
            axis=1,
        )
        y = lax.dot_general(
            lhs[...], rhs, (((1,), (1,)), ((), ())), preferred_element_type=jnp.float32
        )
        y = y.reshape(geo.batch, -1, width)
        at = 0
        for start, many in spans:
            base = cot[:, start : start + many, columns].astype(jnp.float32)
            total = (base + y[:, at : at + many]).astype(jnp.bfloat16)
            tiles[:, at : at + many, columns] = total
            at += many
    at, stores = 0, []
    for n, (start, many) in enumerate(spans):
        here, there = pl.ds(at, many), pl.ds(start, many)
        stores.append(pltpu.make_async_copy(tiles.at[:, here], out.at[:, there], sems.at[n]))
        stores[-1].start()
        at += many
    for store in stores:
        store.wait()


def inner_kernel(geo, place, k1s, ext, cot, out, shifted, lhs, tiles, sems):
    wide, mid, high = geo.wide, geo.mid, geo.high
    count = geo.ext - 4

    def full(kind, part):
        base = (kind * 2 + part) * geo.plane
        plane = ext[pl.ds(base, geo.plane), :].reshape(geo.batch, geo.ext, wide, mid)
        return plane[:, 2 : 2 + count]

    gradient(geo, place, full, (2, count), shifted)
    windows(geo, shifted, [(2, high - 4)], lhs)
    convolve_back(geo, lhs, k1s, cot, [(2 * wide, (high - 4) * wide)], out, tiles, sems)


def outer_kernel(geo, place, k1s, ext, near_strip, next_strip, cot, given, out, shifted, lhs, tiles, sems):
    wide, mid, high = geo.wide, geo.mid, geo.high
    two = (geo.batch, 2, wide, mid)
    even = place[1] % 2 == 0
    for first in (0, geo.ext - 4):
        near = jnp.logical_xor(even, first == 0)

        def full(kind, part):
            base = (kind * 2 + part) * geo.plane
            plane = ext[pl.ds(base, geo.plane), :].reshape(geo.batch, geo.ext, wide, mid)
            plane = plane[:, first : first + 4]
            got = jnp.where(
                near,
                near_strip[kind, part].astype(jnp.float32),
                next_strip[kind, part].astype(jnp.float32),
            ).reshape(two)
            none = jnp.zeros_like(got)
            return plane + jnp.concatenate([none, got] if first else [got, none], axis=1)

        gradient(geo, place, full, (first, 4), shifted)
    windows(geo, shifted, [(0, 2), (high - 2, 2)], lhs)
    spans = [(0, 2 * wide), ((high - 2) * wide, 2 * wide)]
    convolve_back(geo, lhs, k1s, cot, spans, out, tiles, sems)


def second_calls(geo, place, k1, ext, near_strip, next_strip, cot):
    taps = TAPS * TAPS
    image = (geo.batch, geo.high * geo.wide, geo.chan)
    out = jax.ShapeDtypeStruct(image, jnp.bfloat16)
    cot = cot.reshape(image)

    def call(kernel, args, rows, given):
        pixels = rows * geo.wide
        return pl.pallas_call(
            lambda *refs: kernel(geo, *refs),
            out_shape=out,
            in_specs=[smem()] + [whole(a) for a in (*args[1:], cot)] + [far(g) for g in given],
            out_specs=far(out),
            scratch_shapes=[
                pltpu.VMEM((TAPS, geo.batch, geo.ext, geo.wide, geo.mid), jnp.float32),
                pltpu.VMEM((geo.batch * pixels, taps * geo.mid), jnp.bfloat16),
                pltpu.VMEM((geo.batch, pixels, geo.chan), jnp.bfloat16),
                pltpu.SemaphoreType.DMA((2,)),
            ],
            input_output_aliases={len(args) + 1: 0} if given else {},
            compiler_params=pltpu.CompilerParams(vmem_limit_bytes=VMEM_LIMIT),
            cost_estimate=pl.CostEstimate(
                flops=2 * geo.batch * pixels * taps * geo.chan * geo.mid,
                bytes_accessed=2 * taps * geo.chan * geo.mid,
                transcendentals=geo.plane * geo.mid,
            ),
        )(*args, cot, *given)

    inner = call(inner_kernel, [place, k1, ext], geo.high - 4, [])
    return call(outer_kernel, [place, k1, ext, near_strip, next_strip], 4, [inner])


def along_rows(geo, near_strip, next_strip):
    pair = [(i, i ^ 1) for i in range(geo.rows) if i ^ 1 < geo.rows]
    between = [p for i in range(1, geo.rows - 1, 2) for p in ((i, i + 1), (i + 1, i))]
    return lax.ppermute(near_strip, "row", pair), lax.ppermute(next_strip, "row", between)


def shards(inputs, cotangent, w_in, w_out):
    geo = Geometry(inputs, w_in)
    row, col = lax.axis_index("row"), lax.axis_index("col")
    core = col % 2
    x = inputs.reshape(geo.pixels, geo.chan)
    cot = cotangent.reshape(geo.pixels, geo.chan)
    place = jnp.stack([core, row, col]).astype(jnp.int32)
    if geo.pieces_fit():
        groups, found = gather_pieces(geo, w_in, w_out)
        table = chip_table(geo, core)
        weights, (x, cot), pieces = weights_calls(geo, table, groups, found, (x, cot))
        ext, inner, outer, k1, _ = partial_call(geo, table, x, cot, weights, pieces)
    else:
        k1 = lax.all_gather(w_in, AXES, axis=0, tiled=True).reshape(-1, geo.mid)
        k2 = lax.all_gather(w_out, AXES, axis=0, tiled=True).reshape(-1, geo.chan)
        ext, inner, outer = partial_call(geo, place, x, cot, [k1, k2])
    inner, outer = beside(geo, inner, outer)
    full, *strips = join_call(geo, place, ext, inner, outer)
    out = second_calls(geo, place, k1, full, *along_rows(geo, *strips), cot)
    return out.reshape(inputs.shape)


def solution(mesh):
    return jax.shard_map(
        shards,
        mesh=mesh,
        in_specs=(
            P(None, "row", "col", None),
            P(None, "row", "col", None),
            P(("row", "col")),
            P(("row", "col")),
        ),
        out_specs=P(None, "row", "col", None),
        check_vma=False,
    )
```

```python
import jax
import jax.numpy as jnp
from jax import lax
from jax.experimental import pallas as pl
from jax.experimental.pallas import tpu as pltpu
from jax.sharding import PartitionSpec as P

AXES = ("row", "col")
VMEM_LIMIT = 16 * 1024 * 1024
TAPS = 3
PLAN = {
    "far_half": True,
    "modes": {"c": "cat", "d": "sep", "o": "cat"},
    "holds": {"z3": ("z2",)},
    "early": ("o", "c", "d"),
    "pin": True,
    "late": 1,
    "late_c": 0,
    "cut": 1,
    "wait_c": "d2",
    "table": "d2",
    "costs": (0, 0),
}


def is_power(n):
    return n > 0 and n & (n - 1) == 0


def whole(array):
    return pl.BlockSpec(memory_space=pltpu.VMEM)


def far(array):
    return pl.BlockSpec(memory_space=pltpu.HBM)


class Geometry:
    def __init__(self, inputs, w_in):
        self.batch, self.high, self.wide, self.chan = inputs.shape
        self.rows, self.cols = lax.axis_size("row"), lax.axis_size("col")
        self.zs = self.cols // 2
        self.shard = w_in.shape[0]
        self.mid = self.shard * self.rows * self.cols // (TAPS * TAPS * self.chan)
        self.pixels = self.batch * self.high * self.wide
        self.ext = self.high + 2
        self.lines = self.batch * self.ext
        self.plane = self.lines * self.wide
        self.deep1 = self.shard // self.mid
        self.deep2 = self.shard // self.chan
        self.blocks = self.chan // self.mid

    def pieces_fit(self):
        return (
            self.cols % 2 == 0
            and is_power(self.zs)
            and is_power(self.rows)
            and self.rows >= 2
            and self.shard % self.chan == 0
            and self.chan % self.mid == 0
            and (2 * self.deep1) % 16 == 0
            and (4 * self.deep2) % 16 == 0
        )


def device_perm(geo, move):
    pairs = []
    for row in range(geo.rows):
        for col in range(geo.cols):
            r, z, k = move(row, col // 2, col % 2)
            pairs.append((row * geo.cols + col, r * geo.cols + z * 2 + k))
    return pairs


def send(x, perm):
    return lax.ppermute(x, AXES, perm)


def row_bits(geo, core):
    bits = [1 << i for i in range(geo.rows.bit_length() - 1)]
    return bits if core == 0 else bits[::-1]


def row_masks(geo, core):
    masks = [0]
    for bit in row_bits(geo, core):
        masks = masks + [m ^ bit for m in masks]
    return masks


def after(x, *others):
    return lax.optimization_barrier((x, *others))[0]


def double_rows(geo, x, step):
    perm = device_perm(geo, lambda r, z, k: (r ^ row_bits(geo, k)[step], z, k))
    return send(x, perm)


def depth_groups(geo):
    masks = list(range(geo.zs))
    cut = max(1, geo.zs // 2 if PLAN["far_half"] else geo.zs - 1)
    groups = {"o": masks[:1], "c": masks[1:cut], "d": masks[cut:]}
    return {name: group for name, group in groups.items() if group}


def own_part(geo, w_in, w_out):
    def kernel(first, second, out):
        out[0, : geo.deep1] = first[...]
        target = lax.broadcasted_iota(jnp.int32, (geo.deep1, 1), 0)
        block = sum((target >= b * geo.deep2).astype(jnp.int32) for b in range(1, geo.blocks))
        wanted = (target - geo.deep2 * block) * geo.blocks + block
        source = lax.broadcasted_iota(jnp.int32, (geo.deep1, geo.deep1), 1)
        pick = (source == wanted).astype(jnp.bfloat16)
        rows = jnp.dot(pick, second[...], preferred_element_type=jnp.float32)
        out[0, geo.deep1 :] = rows.astype(jnp.bfloat16)

    out = jax.ShapeDtypeStruct((1, 2 * geo.deep1, geo.mid), jnp.bfloat16)
    args = [w.reshape(geo.deep1, geo.mid) for w in (w_in, w_out)]
    return pl.pallas_call(
        kernel,
        out_shape=out,
        in_specs=[whole(a) for a in args],
        out_specs=whole(out),
        compiler_params=parameters(),
    )(*args)


def gather_pieces(geo, w_in, w_out):
    own = own_part(geo, w_in, w_out)
    steps = len(row_bits(geo, 0))
    found = {"z0": own}

    def ready(name, x):
        held = [found[other] for other in PLAN["holds"].get(name, ()) if other in found]
        return after(x, *held) if held else x

    def along_z(mask):
        bit = mask & -mask
        perm = device_perm(geo, lambda r, z, k: (r, z ^ bit, k))
        name = f"z{mask}"
        found[name] = send(ready(name, found[f"z{mask ^ bit}"]), perm)

    def along_rows_of(name, x):
        parts, count = [x], 0
        for step in range(steps):
            if PLAN["modes"][name] == "cat":
                parts = [parts[0] if step == 0 else jnp.concatenate(parts, axis=0)]
            new = []
            for n, part in enumerate(parts):
                key = f"{name}{count}"
                part = ready(key, part)
                if name == "d" and step == steps - 1 and n == len(parts) - 1:
                    found[key] = double_rows(geo, part[:, : geo.deep1], step)
                    new += [found[key], double_rows(geo, part[:, geo.deep1 :], step)]
                else:
                    found[key] = double_rows(geo, part, step)
                    new.append(found[key])
                count += 1
            parts = parts + new
        return parts

    groups = depth_groups(geo)
    if geo.zs > 1:
        along_z(geo.zs // 2)
    done = {"o": along_rows_of("o", own)}
    for mask in sorted(range(1, geo.zs), key=lambda m: (m.bit_count(), m)):
        if mask != geo.zs // 2:
            along_z(mask)
    for name in groups:
        if name != "o":
            parts = [found[f"z{mask}"] for mask in groups[name]]
            x = parts[0] if len(parts) == 1 else jnp.concatenate(parts, axis=0)
            done[name] = along_rows_of(name, x)
    return done, found


def swap_cores(geo, x):
    return send(x, device_perm(geo, lambda r, z, k: (r, z, 1 - k)))


def chip_table(geo, core):
    row = lax.axis_index("row")
    z = lax.axis_index("col") // 2
    table = []
    for group in depth_groups(geo).values():
        depth = z ^ jnp.array(group)[None, :]
        both = [
            ((row ^ jnp.array(row_masks(geo, k))[:, None]) * geo.zs + depth).reshape(-1)
            for k in (0, 1)
        ]
        table += [jnp.where(core == 0, *both), jnp.where(core == 0, *both[::-1])]
    return jnp.concatenate([jnp.asarray([core]), *table]).astype(jnp.int32)


def place_rows(target, base, offset, columns, rows):
    skew = offset % 16
    at = pl.multiple_of(base + (offset - skew), 16)
    if skew:
        rows = jnp.concatenate([target[pl.ds(at, 16), columns][:skew], rows], axis=0)
    target[pl.ds(at, rows.shape[0]), columns] = rows


def place_first(geo, chip, of_core, rows, k1s):
    base = pl.multiple_of(chip * (2 * geo.deep1), 16)
    place_rows(k1s, base, of_core * geo.deep1, slice(0, geo.mid), rows)


def place_second(geo, chip, of_core, rows, k2s):
    base = pl.multiple_of((chip // 2) * (4 * geo.deep2), 16)
    for odd in range(2):

        @pl.when(chip % 2 == odd)
        def _():
            for b in range(geo.blocks):
                columns = slice(b * geo.mid, (b + 1) * geo.mid)
                block = rows[b * geo.deep2 : (b + 1) * geo.deep2]
                offset = (2 * odd + of_core) * geo.deep2
                place_rows(k2s, base, offset, columns, block)


def place_array(geo, table, start, source, ref, k1s, k2s):
    core = table[0]

    @pl.loop(0, ref.shape[0])
    def _(n):
        chip = table[start + n]
        for of_core in range(2):

            @pl.when(core == (source ^ of_core))
            def _():
                if k1s is not None:
                    place_first(geo, chip, of_core, ref[n, : geo.deep1], k1s)
                if k2s is not None:
                    place_second(geo, chip, of_core, ref[n, ref.shape[1] - geo.deep1 :], k2s)


def weights_calls(geo, table, groups, found, tiles):
    start = 1
    entries = {}
    *_, name = groups
    *groups[name], second = groups[name]
    first = groups[name][-1]
    for group, arrays in groups.items():
        total = sum(y.shape[0] for y in arrays)
        at = start
        entries[group] = []
        for y in arrays:
            entries[group].append((at, total, y))
            at += y.shape[0]
        start += 2 * total

    def both(some, wait=None):
        theirs = [
            swap_cores(geo, after(y, wait) if wait is not None and n == len(some) - 1 else y)
            for n, (_, _, y) in enumerate(some)
        ]
        return [(at, 0, y) for at, _, y in some] + [
            (at + total, 1, y) for (at, total, _), y in zip(some, theirs)
        ]

    at, total, _ = entries[name].pop()
    before = []
    if PLAN["late_c"] and len(groups) == 3:
        before = [entries["c"].pop()]
    weights = []
    for names in PLAN["early"]:
        pieces = []
        is_last = names == PLAN["early"][-1]
        loads = tiles if is_last else ()
        here = after(table, found[PLAN["table"]]) if is_last and PLAN["table"] in found else table
        for group in names:
            if entries.get(group):
                pieces += both(entries[group], weights[0] if weights and PLAN["pin"] else None)
        if pieces:
            weights = early_call(geo, here, pieces, weights[:2], loads)
    firsts = both(before, found.get(PLAN["wait_c"]))
    for n in range(0, first.shape[0], PLAN["cut"]):
        firsts += both([(at + n, total, first[n : n + PLAN["cut"]])])
    return weights[:2], weights[2:], firsts, lambda ext: both([(at, total, second)], ext)


def weights_shapes(geo):
    taps = TAPS * TAPS
    return [
        jax.ShapeDtypeStruct((taps * geo.chan, geo.mid), jnp.bfloat16),
        jax.ShapeDtypeStruct((taps * geo.mid, geo.chan), jnp.bfloat16),
    ]


def smem():
    return pl.BlockSpec(memory_space=pltpu.SMEM)


def parameters():
    return pltpu.CompilerParams(vmem_limit_bytes=VMEM_LIMIT)


def early_call(geo, table, pieces, weights, tiles=()):
    arrays = [x for _, _, x in pieces]
    count = len(arrays) + len(weights)

    def kernel(table, *refs):
        sem = refs[-1]
        outs = refs[count + len(tiles) : -1]
        loads = [
            pltpu.make_async_copy(refs[count + n], outs[2 + n], sem.at[n])
            for n in range(len(tiles))
        ]
        for load in loads:
            load.start()
        for (start, source, _), ref in zip(pieces, refs):
            place_array(geo, table, start, source, ref, *outs[:2])
        for load in loads:
            load.wait()

    outs = weights_shapes(geo) + [jax.ShapeDtypeStruct(t.shape, t.dtype) for t in tiles]
    return pl.pallas_call(
        kernel,
        out_shape=outs,
        in_specs=[smem()] + [whole(x) for x in (*arrays, *weights)] + [far(t) for t in tiles],
        out_specs=[whole(o) for o in outs],
        scratch_shapes=[pltpu.SemaphoreType.DMA((2,))],
        input_output_aliases={1 + len(arrays) + n: n for n in range(len(weights))},
        compiler_params=parameters(),
        cost_estimate=pl.CostEstimate(
            flops=0,
            bytes_accessed=PLAN["costs"][0] * 8 * TAPS * TAPS * geo.chan * geo.mid,
            transcendentals=0,
        ),
    )(table, *arrays, *weights, *tiles)


def partial_convolution(geo, kind, weights, tile, ext, acc):
    mid, chan, wide, high = geo.mid, geo.chan, geo.wide, geo.high
    taps = TAPS * TAPS
    shape = (geo.batch, high, wide, mid)
    lane = lax.broadcasted_iota(jnp.int32, (geo.batch, geo.ext, wide, mid), 2)
    acc[...] = jnp.zeros_like(acc)
    for t in range(0, taps, 2):
        many = min(2, taps - t)
        if kind == 0:
            rhs = [weights[(t + n) * chan : (t + n + 1) * chan, :] for n in range(many)]
            rhs = rhs[0] if many == 1 else jnp.concatenate(rhs, axis=1)
            y = jnp.dot(tile[...], rhs, preferred_element_type=jnp.float32)
        else:
            rhs = weights[t * mid : (t + many) * mid, :]
            y = lax.dot_general(
                tile[...], rhs, (((1,), (1,)), ((), ())), preferred_element_type=jnp.float32
            )
        for n in range(many):
            a, e = divmod(t + n, TAPS)
            if kind == 0:
                a, e = TAPS - 1 - a, TAPS - 1 - e
            acc[e, :, a : a + high] += y[:, n * mid : (n + 1) * mid].reshape(shape)
    to_left = pltpu.roll(acc[0], wide - 1, 2)
    to_right = pltpu.roll(acc[2], 1, 2)
    zero = jnp.zeros_like(to_left)
    main = (
        acc[1]
        + jnp.where(lane == wide - 1, zero, to_left)
        + jnp.where(lane == 0, zero, to_right)
    )
    side = jnp.where(lane == wide - 1, to_left, zero) + jnp.where(lane == 0, to_right, zero)
    ext[pl.ds(0, geo.plane), :] = main.reshape(geo.plane, mid)
    ext[pl.ds(geo.plane, geo.plane), :] = side.reshape(geo.plane, mid)


def column(geo, ext, part, j):
    return ext[pl.ds(part * geo.plane + j, geo.lines, stride=geo.wide), :]


def first_call(geo, table, x, weights, pieces=()):
    ext = jax.ShapeDtypeStruct((2 * geo.plane, geo.mid), jnp.float32)
    arrays = [y for _, _, y in pieces]

    def kernel(table, x, *refs):
        acc = refs[-1]
        if pieces:
            ext, k1s, k2s = refs[-4:-1]
            for (start, source, _), ref in zip(pieces, refs):
                both = ref.shape[1] > geo.deep1
                place_array(geo, table, start, source, ref, k1s, k2s if both else None)
        else:
            k1s, ext = refs[0], refs[-2]
        partial_convolution(geo, 0, k1s, x, ext, acc)

    args = [table, x, *arrays, *weights]
    outs = [ext] + (weights_shapes(geo) if pieces else [])
    alias = {2 + len(arrays) + n: 1 + n for n in range(len(weights))}
    return pl.pallas_call(
        kernel,
        out_shape=outs,
        in_specs=[smem()] + [whole(a) for a in args[1:]],
        out_specs=[whole(o) for o in outs],
        scratch_shapes=[pltpu.VMEM((TAPS, geo.batch, geo.ext, geo.wide, geo.mid), jnp.float32)],
        input_output_aliases=alias if pieces else {},
        compiler_params=parameters(),
        cost_estimate=pl.CostEstimate(
            flops=PLAN["costs"][1] * 2 * geo.pixels * TAPS * TAPS * geo.chan * geo.mid,
            bytes_accessed=PLAN["costs"][1] * 2 * TAPS * TAPS * geo.chan * geo.mid,
            transcendentals=0,
        ),
    )(*args)


def back_call(geo, table, cot, ext_pre, k2, pieces=()):
    ext = jax.ShapeDtypeStruct((2 * geo.plane, geo.mid), jnp.float32)
    edge = jax.ShapeDtypeStruct((2, 2, geo.lines, geo.mid), jnp.bfloat16)
    arrays = [x for _, _, x in pieces]
    count = len(arrays)

    def kernel(table, cot, ext_pre, *refs):
        ext, inner, outer = refs[count + 1 : count + 4]
        k2s = refs[-2] if count else refs[0]
        for (start, source, _), ref in zip(pieces, refs):
            place_array(geo, table, start, source, ref, None, k2s)
        partial_convolution(geo, 1, k2s, cot, ext, refs[-1])
        left, right = ((1, geo.wide - 1), (0, 0)), ((0, geo.wide - 1), (1, 0))
        core = table[0]
        for out, is_right in ((inner, core == 0), (outer, core != 0)):
            for kind, plane in enumerate((ext_pre, ext)):
                for n in range(2):
                    value = jnp.where(
                        is_right, column(geo, plane, *right[n]), column(geo, plane, *left[n])
                    )
                    out[kind, n] = value.astype(jnp.bfloat16)

    outs = [ext, edge, edge] + (weights_shapes(geo)[1:] if count else [])
    args = [table, cot, ext_pre, *arrays, k2]
    return pl.pallas_call(
        kernel,
        out_shape=outs,
        in_specs=[smem()] + [whole(a) for a in args[1:]],
        out_specs=[whole(o) for o in outs],
        scratch_shapes=[pltpu.VMEM((TAPS, geo.batch, geo.ext, geo.wide, geo.mid), jnp.float32)],
        input_output_aliases={3 + count: 3} if count else {},
        compiler_params=parameters(),
        cost_estimate=pl.CostEstimate(
            flops=2 * geo.pixels * TAPS * TAPS * geo.chan * geo.mid,
            bytes_accessed=2 * TAPS * TAPS * geo.chan * geo.mid,
            transcendentals=0,
        ),
    )(*args)[:3]


def beside(geo, inner, outer):
    swap = device_perm(geo, lambda r, z, k: (r, z, 1 - k))
    pairs = []
    for row in range(geo.rows):
        for col in range(1, geo.cols - 1, 2):
            a, b = row * geo.cols + col, row * geo.cols + col + 1
            pairs += [(a, b), (b, a)]
    return send(inner, swap), send(outer, pairs)


def join_call(geo, place, ext_pre, ext_back, inner, outer):
    full = jax.ShapeDtypeStruct((2 * geo.plane, geo.mid), jnp.float32)
    strip = jax.ShapeDtypeStruct((2, 2, geo.batch, 2 * geo.wide, geo.mid), jnp.bfloat16)

    def kernel(place, _, __, inner, outer, pre, back, near_strip, next_strip):
        core = place[0]
        even = place[1] % 2 == 0
        wide = geo.wide
        for kind, full in enumerate((pre, back)):

            def add(part, j, value):
                at = pl.ds(part * geo.plane + j, geo.lines, stride=wide)
                full[at, :] = full[at, :] + value

            near = [inner[kind, n].astype(jnp.float32) for n in range(2)]
            next_ = [outer[kind, n].astype(jnp.float32) for n in range(2)]
            left = [jnp.where(core == 0, b, a) for a, b in zip(near, next_)]
            right = [jnp.where(core == 0, a, b) for a, b in zip(near, next_)]
            add(1, wide - 1, left[0])
            add(0, 0, left[1])
            add(0, wide - 1, right[0])
            add(1, 0, right[1])
            for part in range(2):
                for b in range(geo.batch):
                    top = part * geo.plane + b * geo.ext * wide
                    for out, low in ((near_strip, even), (next_strip, jnp.logical_not(even))):
                        line = pl.multiple_of(top + jnp.where(low, geo.high * wide, 0), 8)
                        two = full[pl.ds(line, 2 * wide), :]
                        out[kind, part, b] = two.astype(jnp.bfloat16)

    args = [place, ext_pre, ext_back, inner, outer]
    return pl.pallas_call(
        kernel,
        out_shape=[full, full, strip, strip],
        in_specs=[smem()] + [whole(a) for a in args[1:]],
        out_specs=[whole(o) for o in (full, full, strip, strip)],
        input_output_aliases={1: 0, 2: 1},
        compiler_params=parameters(),
    )(*args)


def gradient(geo, place, full, lines, shifted):
    mid, wide = geo.mid, geo.wide
    f32 = jnp.float32
    first, count = lines
    shape = (geo.batch, count, wide, mid)
    line = lax.broadcasted_iota(jnp.int32, shape, 1) + first
    lane = lax.broadcasted_iota(jnp.int32, shape, 2)
    row, col = place[1], place[2]
    inside = jnp.logical_and(
        jnp.logical_or(line > 0, row > 0),
        jnp.logical_or(line < geo.ext - 1, row < geo.rows - 1),
    )
    beside = jnp.logical_or(
        jnp.logical_and(lane == wide - 1, col > 0),
        jnp.logical_and(lane == 0, col < geo.cols - 1),
    )
    grads = []
    for part, keep in enumerate((inside, jnp.logical_and(inside, beside))):
        pre, back = full(0, part), full(1, part)
        s = jax.nn.sigmoid(pre)
        grad = back * (s * (1.0 + pre * (1.0 - s)))
        grad = jnp.where(keep, grad, jnp.zeros_like(grad))
        grads.append(grad.astype(jnp.bfloat16).astype(f32))
    main, side = grads
    left = jnp.where(
        lane == wide - 1, pltpu.roll(side, wide - 1, 2), pltpu.roll(main, wide - 1, 2)
    )
    right = jnp.where(lane == 0, pltpu.roll(side, 1, 2), pltpu.roll(main, 1, 2))
    for e, value in enumerate((left, main, right)):
        shifted[e, :, first : first + count] = value


def windows(geo, shifted, spans, lhs):
    for t in range(TAPS * TAPS):
        a, e = divmod(t, TAPS)
        parts = []
        for first, count in spans:
            at = first + TAPS - 1 - a
            parts.append(shifted[e, :, at : at + count])
        window = parts[0] if len(parts) == 1 else jnp.concatenate(parts, axis=1)
        window = window.reshape(-1, geo.mid).astype(jnp.bfloat16)
        lhs[:, t * geo.mid : (t + 1) * geo.mid] = window


def convolve_back(geo, lhs, k1s, cot, spans, out, tiles, sems):
    width = 2 * geo.mid
    for n in range(geo.chan // width):
        columns = slice(n * width, (n + 1) * width)
        rhs = jnp.concatenate(
            [
                k1s[t * geo.chan + n * width : t * geo.chan + (n + 1) * width, :]
                for t in range(TAPS * TAPS)
            ],
            axis=1,
        )
        y = lax.dot_general(
            lhs[...], rhs, (((1,), (1,)), ((), ())), preferred_element_type=jnp.float32
        )
        y = y.reshape(geo.batch, -1, width)
        at = 0
        for start, many in spans:
            base = cot[:, start : start + many, columns].astype(jnp.float32)
            total = (base + y[:, at : at + many]).astype(jnp.bfloat16)
            tiles[:, at : at + many, columns] = total
            at += many
    at, stores = 0, []
    for n, (start, many) in enumerate(spans):
        here, there = pl.ds(at, many), pl.ds(start, many)
        stores.append(pltpu.make_async_copy(tiles.at[:, here], out.at[:, there], sems.at[n]))
        stores[-1].start()
        at += many
    for store in stores:
        store.wait()


def inner_kernel(geo, place, k1s, pre, back, cot, out, shifted, lhs, tiles, sems):
    wide, mid, high = geo.wide, geo.mid, geo.high
    exts = (pre, back)
    count = geo.ext - 4

    def full(kind, part):
        plane = exts[kind][pl.ds(part * geo.plane, geo.plane), :].reshape(geo.batch, geo.ext, wide, mid)
        return plane[:, 2 : 2 + count]

    gradient(geo, place, full, (2, count), shifted)
    windows(geo, shifted, [(2, high - 4)], lhs)
    convolve_back(geo, lhs, k1s, cot, [(2 * wide, (high - 4) * wide)], out, tiles, sems)


def outer_kernel(geo, place, k1s, pre, back, near_strip, next_strip, cot, given, out, shifted, lhs, tiles, sems):
    wide, mid, high = geo.wide, geo.mid, geo.high
    exts = (pre, back)
    two = (geo.batch, 2, wide, mid)
    even = place[1] % 2 == 0
    for first in (0, geo.ext - 4):
        near = jnp.logical_xor(even, first == 0)

        def full(kind, part):
            plane = exts[kind][pl.ds(part * geo.plane, geo.plane), :].reshape(geo.batch, geo.ext, wide, mid)
            plane = plane[:, first : first + 4]
            got = jnp.where(
                near,
                near_strip[kind, part].astype(jnp.float32),
                next_strip[kind, part].astype(jnp.float32),
            ).reshape(two)
            none = jnp.zeros_like(got)
            return plane + jnp.concatenate([none, got] if first else [got, none], axis=1)

        gradient(geo, place, full, (first, 4), shifted)
    windows(geo, shifted, [(0, 2), (high - 2, 2)], lhs)
    spans = [(0, 2 * wide), ((high - 2) * wide, 2 * wide)]
    convolve_back(geo, lhs, k1s, cot, spans, out, tiles, sems)


def second_calls(geo, place, k1, pre, back, near_strip, next_strip, cot):
    taps = TAPS * TAPS
    image = (geo.batch, geo.high * geo.wide, geo.chan)
    out = jax.ShapeDtypeStruct(image, jnp.bfloat16)
    cot = cot.reshape(image)

    def call(kernel, args, rows, given):
        pixels = rows * geo.wide
        return pl.pallas_call(
            lambda *refs: kernel(geo, *refs),
            out_shape=out,
            in_specs=[smem()] + [whole(a) for a in (*args[1:], cot)] + [far(g) for g in given],
            out_specs=far(out),
            scratch_shapes=[
                pltpu.VMEM((TAPS, geo.batch, geo.ext, geo.wide, geo.mid), jnp.float32),
                pltpu.VMEM((geo.batch * pixels, taps * geo.mid), jnp.bfloat16),
                pltpu.VMEM((geo.batch, pixels, geo.chan), jnp.bfloat16),
                pltpu.SemaphoreType.DMA((2,)),
            ],
            input_output_aliases={len(args) + 1: 0} if given else {},
            compiler_params=pltpu.CompilerParams(vmem_limit_bytes=VMEM_LIMIT),
            cost_estimate=pl.CostEstimate(
                flops=2 * geo.batch * pixels * taps * geo.chan * geo.mid,
                bytes_accessed=2 * taps * geo.chan * geo.mid,
                transcendentals=geo.plane * geo.mid,
            ),
        )(*args, cot, *given)

    inner = call(inner_kernel, [place, k1, pre, back], geo.high - 4, [])
    return call(outer_kernel, [place, k1, pre, back, near_strip, next_strip], 4, [inner])


def along_rows(geo, near_strip, next_strip):
    pair = [(i, i ^ 1) for i in range(geo.rows) if i ^ 1 < geo.rows]
    between = [p for i in range(1, geo.rows - 1, 2) for p in ((i, i + 1), (i + 1, i))]
    return lax.ppermute(near_strip, "row", pair), lax.ppermute(next_strip, "row", between)


def shards(inputs, cotangent, w_in, w_out):
    geo = Geometry(inputs, w_in)
    row, col = lax.axis_index("row"), lax.axis_index("col")
    core = col % 2
    x = inputs.reshape(geo.pixels, geo.chan)
    cot = cotangent.reshape(geo.pixels, geo.chan)
    place = jnp.stack([core, row, col]).astype(jnp.int32)
    if geo.pieces_fit():
        groups, found = gather_pieces(geo, w_in, w_out)
        table = chip_table(geo, core)
        weights, (x, cot), firsts, seconds = weights_calls(geo, table, groups, found, (x, cot))
        ext_pre, k1, k2 = first_call(geo, table, x, weights, firsts)
        ext_back, inner, outer = back_call(geo, table, cot, ext_pre, k2, seconds(ext_pre))
    else:
        k1 = lax.all_gather(w_in, AXES, axis=0, tiled=True).reshape(-1, geo.mid)
        k2 = lax.all_gather(w_out, AXES, axis=0, tiled=True).reshape(-1, geo.chan)
        (ext_pre,) = first_call(geo, place, x, [k1])
        ext_back, inner, outer = back_call(geo, place, cot, ext_pre, k2)
    inner, outer = beside(geo, inner, outer)
    pre, back, *strips = join_call(geo, place, ext_pre, ext_back, inner, outer)
    out = second_calls(geo, place, k1, pre, back, *along_rows(geo, *strips), cot)
    return out.reshape(inputs.shape)


def solution(mesh):
    return jax.shard_map(
        shards,
        mesh=mesh,
        in_specs=(
            P(None, "row", "col", None),
            P(None, "row", "col", None),
            P(("row", "col")),
            P(("row", "col")),
        ),
        out_specs=P(None, "row", "col", None),
        check_vma=False,
    )
```
